256 devices in a mesh: lon: 16 (over z_lo, y), lat: 16 (over x, z_hi, core).
Axes of the slice: x: 4, y: 4, z: 8 (z_hi: 2, z_lo: 4; z = z_hi * 4 + z_lo), core: 2. Of those that a mesh axis runs over, the one named last changes fastest.
Arguments:
- sample_deviations: float32 [32, 32, 128, 2048], P(None, None, 'lat', 'lon'), may hold values from -6 to 6
- east_courant: float32 [32, 128, 2048], P(None, 'lat', 'lon'), may hold values from -0.45 to 0.45
- north_courant: float32 [32, 128, 2048], P(None, 'lat', 'lon'), may hold values from -0.45 to 0.45
- production: float32 [32, 128, 2048], P(None, 'lat', 'lon'), may hold values from -1.8 to 1.8
- loss_rate: float32 [32, 128, 2048], P(None, 'lat', 'lon'), may hold values from 0.02 to 0.3
- entry_count: int32 [256], P(('lon', 'lat')), may hold values from 24 to 48, as said below
- entry_row: int32 [12288], P(('lon', 'lat')), may hold values from 0 to 7
- entry_block: int32 [12288], P(('lon', 'lat')), may hold values from 0 to 63
- path_weight: bfloat16 [12288, 128, 128], P(('lon', 'lat')), may hold values from 0 to 0.15234375
- observed: float32 [131072], P(('lon', 'lat')), may hold values from -288 to 288
- obs_var: float32 [131072], P(('lon', 'lat')), may hold values from 512 to 36864, as said below
Outputs:
- updated_samples: float32 [32, 32, 128, 2048], P(None, None, 'lat', 'lon')
- prior_samples_in_path_space: float32 [32, 131072], P(None, ('lon', 'lat'))
- scaled_innovation: float32 [131072], P(('lon', 'lat'))
The draws below stay inside these ranges and needn't reach their ends.
Inputs may be any that keep to these rules, and one draw needn't show every extreme that they name: `entry_count`: live crossing slots of each tile; some tile has all 48 live in every draw. `obs_var`: positive.
All inputs are finite; a program needn't handle non-finite values.
Results may differ from the reference program's by a relative error of at most 0.0025.
Values sent between devices are 32-bit elements; how exact they have to be, the bound alone decides.
A program may use at most 64 MiB of HBM per device.

```python
import math
import jax
import jax.numpy as jnp
from jax import lax

SAMPLE_TOTAL = 32
ALTITUDE_LAYERS = 32
TILE_LAT = 8
TILE_LON = 128
RAY_BLOCK = 128
BLOCKS_DEV = 4
SLOTS_TILE = 48
GRID_LAT = 128
GRID_LON = 2048
COL_BLOCKS = 64
TILES = 256
RAYS = 131072
SLOTS = 12288


def draw_entry_count(key, part):
    tiles_lat = GRID_LAT // TILE_LAT
    tile_ids = jnp.arange(TILES)
    lat_pos = tile_ids % tiles_lat
    lower = SLOTS_TILE // 2
    upper = SLOTS_TILE + 1
    random_counts = jax.random.randint(key, (TILES,), lower, upper)
    return jnp.where(lat_pos == tiles_lat // 2, SLOTS_TILE, random_counts).astype(jnp.int32)


def draw_obs_var(key, part):
    per_tile = BLOCKS_DEV * RAY_BLOCK
    ray_ids = jnp.arange(RAYS)
    position = (ray_ids // per_tile).astype(jnp.float32) / max(TILES - 1, 1)
    baseline = RAYS / 256.0 * jnp.power(3.0, position)
    spread_factor = jnp.exp(jax.random.uniform(key, (RAYS,), jnp.float32, 0.0, math.log(8.0)))
    return (baseline * spread_factor).astype(jnp.float32)


def touch_ends(values, own_key, least, largest):
    extent = values.shape
    place = [jax.random.randint(jax.random.fold_in(own_key, axis), (), 0, extent[axis]) for axis in range(len(extent))]
    values = values.at[tuple(place)].set(least)
    longest = extent.index(max(extent))
    place[longest] = (place[longest] + 1) % extent[longest]
    return values.at[tuple(place)].set(largest)


def shard_levels(stream_key, extent, split, least, high):
    def one(dim, parts):
        heights = jax.random.uniform(jax.random.fold_in(jax.random.fold_in(stream_key, 6), dim), (parts,), jnp.float32, least / len(split), high / len(split))
        return jnp.repeat(jnp.exp(heights), extent[dim] // parts).reshape((-1,) + (1,) * (len(extent) - dim - 1))

    loudness = one(*split[0])
    for cut in split[1:]:
        loudness = loudness * one(*cut)
    return loudness


def normal_values(key, extent, width, reach, pieces=(), held_as=jnp.bfloat16):
    result = jax.random.normal(key, extent, jnp.float32) * width
    if len(pieces) > 0:
        result = shard_levels(key, extent, pieces, -0.22, 0.18) * result
    return jnp.clip(result, min=-reach, max=reach).astype(held_as)


def setup_inputs(seed: int = 0) -> dict:
    streams_of = jax.random.split(jax.random.key(seed), 12)
    sample_deviations = normal_values(streams_of[0], (SAMPLE_TOTAL, ALTITUDE_LAYERS, GRID_LAT, GRID_LON), 1.0, 6.0, ((2, 16), (3, 16)), jnp.float32)
    east_courant = jnp.clip(jax.random.uniform(streams_of[1], (ALTITUDE_LAYERS, GRID_LAT, GRID_LON), jnp.float32, -0.45, 0.45) * shard_levels(streams_of[1], (ALTITUDE_LAYERS, GRID_LAT, GRID_LON), ((1, 16), (2, 16)), -0.4, 0.0), -0.45, 0.45)
    north_courant = jnp.clip(jax.random.uniform(streams_of[2], (ALTITUDE_LAYERS, GRID_LAT, GRID_LON), jnp.float32, -0.45, 0.45) * shard_levels(streams_of[2], (ALTITUDE_LAYERS, GRID_LAT, GRID_LON), ((1, 16), (2, 16)), -0.4, 0.0), -0.45, 0.45)
    production = normal_values(streams_of[3], (ALTITUDE_LAYERS, GRID_LAT, GRID_LON), 0.3, 1.8, ((1, 16), (2, 16)), jnp.float32)
    loss_rate = jnp.clip(jnp.exp(math.log(0.3) - 2.7080503 * jax.random.uniform(streams_of[4], (ALTITUDE_LAYERS, GRID_LAT, GRID_LON), jnp.float32) ** shard_levels(streams_of[4], (ALTITUDE_LAYERS, GRID_LAT, GRID_LON), ((1, 16), (2, 16)), -0.2, 0.2)), 0.02, 0.3)
    entry_count = draw_entry_count(jax.random.fold_in(streams_of[11], 71), 0)
    entry_row = touch_ends(jax.random.randint(streams_of[6], (SLOTS,), 0, TILE_LAT), jax.random.fold_in(streams_of[6], 1), 0, TILE_LAT - 1).astype(jnp.int32)
    entry_block = touch_ends(jax.random.randint(streams_of[7], (SLOTS,), 0, COL_BLOCKS), jax.random.fold_in(streams_of[7], 1), 0, COL_BLOCKS - 1).astype(jnp.int32)
    path_weight = jnp.clip(0.15234375 * jax.random.uniform(streams_of[8], (SLOTS, TILE_LON, RAY_BLOCK), jnp.float32) ** shard_levels(streams_of[8], (SLOTS, TILE_LON, RAY_BLOCK), ((0, 256),), -0.2, 0.2), 0.0, 0.15234375).astype(jnp.bfloat16)
    observed = normal_values(streams_of[9], (RAYS,), 48.0, 288.0, ((0, 256),), jnp.float32)
    obs_var = draw_obs_var(jax.random.fold_in(streams_of[11], 71), 0)
    return dict(sample_deviations=sample_deviations, east_courant=east_courant, north_courant=north_courant, production=production, loss_rate=loss_rate, entry_count=entry_count, entry_row=entry_row, entry_block=entry_block, path_weight=path_weight, observed=observed, obs_var=obs_var)


highest = lax.Precision.HIGHEST

def advance(plasma_concentration, east_speed, north_speed, source, loss_rate):
    west_cell = jnp.roll(plasma_concentration, 1, axis=2)
    east_cell = jnp.roll(plasma_concentration, -1, axis=2)
    padded = jnp.pad(plasma_concentration, ((0, 0), (1, 1), (0, 0)))
    south_cell = padded[:, :-2, :]
    north_cell = padded[:, 2:, :]
    advected = plasma_concentration - jnp.maximum(east_speed, 0.0) * (plasma_concentration - west_cell) - jnp.minimum(east_speed, 0.0) * (east_cell - plasma_concentration)
    advected = advected - jnp.maximum(north_speed, 0.0) * (plasma_concentration - south_cell) - jnp.minimum(north_speed, 0.0) * (north_cell - plasma_concentration)
    return (1.0 - loss_rate) * advected + source

def analysis_weights(gram_sum, pull_sum):
    member_total = gram_sum.shape[0]
    identity = jnp.eye(member_total, dtype=gram_sum.dtype)
    factor_low = jnp.linalg.cholesky(gram_sum + (member_total - 1.0) * identity)
    halfway = lax.linalg.triangular_solve(factor_low, pull_sum[:, None], left_side=True, lower=True)
    mean_weights = lax.linalg.triangular_solve(factor_low, halfway, left_side=True, lower=True, transpose_a=True)
    inverse = lax.linalg.triangular_solve(factor_low, identity, left_side=True, lower=True)
    return mean_weights + math.sqrt(member_total - 1.0) * inverse.T

def reference(sample_deviations, east_courant, north_courant, production, loss_rate, entry_count, entry_row, entry_block, path_weight, observed, obs_var):

    def prior_sample(plasma_concentration):
        first_pass = advance(plasma_concentration, east_courant, north_courant, production, loss_rate)
        return advance(first_pass, east_courant, north_courant, production, loss_rate)
    prior_sample_set = lax.map(prior_sample, sample_deviations)
    column_integral_total = (lax.optimization_barrier(jnp.sum(prior_sample_set, axis=1)) / math.sqrt(ALTITUDE_LAYERS)).astype(jnp.bfloat16)
    tiles_lat = GRID_LAT // TILE_LAT
    rays_column = COL_BLOCKS * RAY_BLOCK
    slot_ids = jnp.arange(SLOTS_TILE, dtype=jnp.int32)
    block_ids = jnp.arange(COL_BLOCKS, dtype=jnp.int32)

    def tile_step(ray_total, tile_index):
        lon_pos = tile_index // tiles_lat
        lat_pos = tile_index % tiles_lat
        tile_patch = lax.dynamic_slice(column_integral_total, (jnp.int32(0), (lat_pos * TILE_LAT).astype(jnp.int32), (lon_pos * TILE_LON).astype(jnp.int32)), (SAMPLE_TOTAL, TILE_LAT, TILE_LON))
        slot_start = (tile_index * SLOTS_TILE).astype(jnp.int32)
        slot_rows = lax.dynamic_slice_in_dim(entry_row, slot_start, SLOTS_TILE)
        slot_blocks = lax.dynamic_slice_in_dim(entry_block, slot_start, SLOTS_TILE)
        slot_weights = lax.dynamic_slice_in_dim(path_weight, slot_start, SLOTS_TILE, 0)
        live_slots = (slot_ids < entry_count[tile_index]).astype(jnp.float32)
        picked = jnp.take(tile_patch, slot_rows, axis=1)
        partial_value = jnp.einsum('mkc,kcr->kmr', picked.astype(jnp.float32), slot_weights.astype(jnp.float32), precision=highest)
        slot_select = (slot_blocks[None, :] == block_ids[:, None]).astype(jnp.float32) * live_slots[None, :]
        summed = jnp.einsum('bk,kmr->mbr', slot_select, partial_value, precision=highest).reshape(SAMPLE_TOTAL, rays_column)
        ray_start = (lon_pos * rays_column).astype(jnp.int32)
        current = lax.dynamic_slice_in_dim(ray_total, ray_start, rays_column, 1)
        return (lax.dynamic_update_slice_in_dim(ray_total, current + summed, ray_start, 1), None)
    prior_samples_in_path_space, _ = lax.scan(tile_step, jnp.zeros((SAMPLE_TOTAL, RAYS), jnp.float32), jnp.arange(TILES, dtype=jnp.int32))
    ray_mean = lax.optimization_barrier(jnp.mean(prior_samples_in_path_space, axis=0))
    spread = prior_samples_in_path_space - ray_mean
    misfit = observed - ray_mean
    scaled_innovation = misfit / jnp.sqrt(obs_var)
    gram_sum = jnp.dot(spread / obs_var, spread.T, precision=highest)
    pull_sum = jnp.dot(spread, misfit / obs_var, precision=highest)
    transform = analysis_weights(gram_sum, pull_sum)
    raveled_grid_vector = prior_sample_set.reshape(SAMPLE_TOTAL, -1)
    centre = lax.optimization_barrier(jnp.mean(raveled_grid_vector, axis=0))
    anomalies = raveled_grid_vector - centre
    updated_samples = centre + jnp.dot(transform.T, anomalies, precision=highest)
    return (updated_samples.reshape(prior_sample_set.shape), prior_samples_in_path_space, scaled_innovation)
```

```python
import math

import jax
import jax.numpy as jnp
from jax import lax
from jax.experimental import pallas as pl
from jax.experimental.pallas import tpu as pltpu
from jax.sharding import PartitionSpec as P

MEMBERS = 32
LEVELS = 32
TILE_LAT = 8
LANES = 128
SLOTS_TILE = 48
COL_BLOCKS = 64
MESH = pl.DeviceIdType.MESH
VMEM = pltpu.VMEM
F32 = jnp.float32
BF16 = jnp.bfloat16


def extended(x, sides, width, wrap):
    for axis, dim in sides:
        size, length = (lax.axis_size(axis), x.shape[dim])
        up = [(i, (i + 1) % size) for i in range(size if wrap else size - 1)]
        down = [(j, i) for i, j in up]
        last = lax.slice_in_dim(x, length - width, length, axis=dim)
        initial = lax.slice_in_dim(x, 0, width, axis=dim)
        before = lax.ppermute(last, axis, up)
        after = lax.ppermute(initial, axis, down)
        x = jnp.concatenate([before, x, after], axis=dim)
    return x


def advance(n, west, east, south, north, east_speed, north_speed, source, loss_rate):
    advected = n - jnp.maximum(east_speed, 0.0) * (n - west) - jnp.minimum(east_speed, 0.0) * (east - n)
    advected = advected - jnp.maximum(north_speed, 0.0) * (n - south) - jnp.minimum(north_speed, 0.0) * (north - n)
    return (1.0 - loss_rate) * advected + source


def ray_kernel(count_ref, row_ref, block_ref, content_ref, weight_ref, summed_ref, part_ref):
    summed_ref[...] = jnp.zeros_like(summed_ref)
    for k in range(SLOTS_TILE):
        picked = content_ref[row_ref[k]]
        part_ref[k] = jnp.dot(picked, weight_ref[k], preferred_element_type=F32)
    for k in range(SLOTS_TILE):
        block = block_ref[k]
        live = k < count_ref[0]
        summed_ref[block] += jnp.where(live, part_ref[k], 0.0)


def ray_sums(entry_count, entry_row, entry_block, content, path_weight):
    smem = pl.BlockSpec(memory_space=pltpu.SMEM)
    vmem = pl.BlockSpec(memory_space=VMEM)
    return pl.pallas_call(
        ray_kernel,
        out_shape=jax.ShapeDtypeStruct((COL_BLOCKS, MEMBERS, LANES), F32),
        in_specs=[smem, smem, smem, vmem, vmem],
        out_specs=vmem,
        scratch_shapes=[VMEM((SLOTS_TILE, MEMBERS, LANES), F32)],
        compiler_params=pltpu.CompilerParams(vmem_limit_bytes=16 * 2**20),
        name="ray_sums",
    )(entry_count, entry_row, entry_block, content, path_weight)


def weights_from(total):
    rows = lax.broadcasted_iota(jnp.int32, (MEMBERS, LANES), 0)
    lanes = lax.broadcasted_iota(jnp.int32, (MEMBERS, LANES), 1)
    inverse_lanes = (lanes >= 64) & (lanes < 64 + MEMBERS)
    work = total + jnp.where(lanes == rows, MEMBERS - 1.0, 0.0) + jnp.where(lanes == rows + 64, 1.0, 0.0)
    for j in range(MEMBERS):
        column = jnp.broadcast_to(work[:, j : j + 1], (MEMBERS, LANES))
        pivot = column[j : j + 1, :]
        scale = jnp.where(rows > j, column, 0.0) * (1.0 / pivot)
        work = work - scale * work[j : j + 1, :]
    diagonal = jnp.sum(jnp.where(lanes == rows, work, 0.0), axis=1, keepdims=True)
    work = work / jnp.sqrt(diagonal)
    inverse = jnp.where(inverse_lanes, work, 0.0)
    halfway = work[:, MEMBERS : MEMBERS + 1]
    mean_weights = jnp.sum(inverse * halfway, axis=0, keepdims=True)
    transform = jnp.where(inverse_lanes, mean_weights + math.sqrt(MEMBERS - 1.0) * inverse, 0.0)
    rest = (1.0 - jnp.sum(transform, axis=1, keepdims=True)) * (1.0 / MEMBERS)
    return jnp.where(inverse_lanes, transform + rest, 0.0)


def analysis_kernel(
    summed_ref, observed_ref, var_ref, prior_ref, innovation_ref, weights_ref,
    own, from_core, from_x, half, from_z, g0, g1, g2, g3, r_core, r_x, r_y, r_z,
    own_sem, core_send, core_recv, x_send, x_recv, z_send, z_recv, a_send, a_recv,
):
    lon, lat = lax.axis_index("lon"), lax.axis_index("lat")
    x, z_hi, core = lat // 4, lax.rem(lat // 2, 2), lax.rem(lat, 2)
    z_lo, y = lon // 4, lax.rem(lon, 4)

    def x_peer(k):
        return (lon, lax.rem(lat + 4 * k, 16))

    def y_peer(k):
        return (z_lo * 4 + lax.rem(y + k, 4), lat)

    def z_peer(k):
        z = lax.rem(z_hi * 4 + z_lo + k, 8)
        return (lax.rem(z, 4) * 4 + y, x * 4 + (z // 4) * 2 + core)

    core_peer = (lon, lat + 1 - 2 * core)
    peers = [core_peer] + [x_peer(k) for k in (1, 2, 3)] + [y_peer(k) for k in (1, 2, 3)]
    peers += [z_peer(k) for k in range(1, 8)]
    barrier = pltpu.get_barrier_semaphore()
    for peer in peers:
        pl.semaphore_signal(barrier, inc=1, device_id=peer, device_id_type=MESH)
    order = (2, 1, 3, 0)
    local = []
    for j in order:
        copy = pltpu.make_async_copy(summed_ref.at[lax.rem(x + j, 4), :, core], own.at[j], own_sem.at[j])
        copy.start()
        local.append(copy)
    pl.semaphore_wait(barrier, len(peers))

    def send(src, dst, send_sem, recv_sem, peer):
        copy = pltpu.make_async_remote_copy(
            src_ref=src, dst_ref=dst, send_sem=send_sem, recv_sem=recv_sem, device_id=peer, device_id_type=MESH
        )
        copy.start()
        return copy

    core_copies = [
        send(summed_ref.at[lax.rem(x + j, 4), :, 1 - core], from_core.at[j], core_send.at[j], core_recv.at[j], core_peer)
        for j in order
    ]
    x_copies = []
    for i, j in enumerate(order):
        local[i].wait()
        core_copies[i].wait_recv()
        own[j] = own[j] + from_core[j]
        if j:
            x_copies.append(send(own.at[j], from_x.at[j - 1], x_send.at[j - 1], x_recv.at[j - 1], x_peer(j)))
    for copy in x_copies:
        copy.wait_recv()
    half[...] = own[0] + from_x[0] + from_x[1] + from_x[2]
    z_copy = send(half.at[1 - z_hi], from_z, z_send, z_recv, z_peer(4))
    z_copy.wait_recv()
    samples = half[z_hi] + from_z[...]

    spreads, scaled = [], []
    for b in range(4):
        block = samples[b * MEMBERS : (b + 1) * MEMBERS]
        prior_ref[:, b * LANES : (b + 1) * LANES] = block
        mean = jnp.sum(block, axis=0, keepdims=True) * (1.0 / MEMBERS)
        misfit = observed_ref[b : b + 1, :] - mean
        variance = var_ref[b : b + 1, :]
        innovation_ref[b : b + 1, :] = misfit / jnp.sqrt(variance)
        spread = block - mean
        spreads.append(jnp.concatenate([spread, jnp.broadcast_to(misfit, (MEMBERS, LANES)), jnp.zeros((64, LANES), F32)], axis=0))
        scaled.append(spread / variance)
    gram = lax.dot_general(
        jnp.concatenate(scaled, axis=1), jnp.concatenate(spreads, axis=1), (((1,), (1,)), ((), ())),
        precision=lax.Precision.HIGHEST, preferred_element_type=F32,
    )
    lanes = lax.broadcasted_iota(jnp.int32, (MEMBERS, LANES), 1)
    g0[...] = jnp.where(lanes <= MEMBERS, gram, 0.0)

    waits = []
    base = 0

    def exchange(source, landing, targets):
        nonlocal base
        copies = [
            send(source, landing.at[i], a_send.at[base + i], a_recv.at[base + i], target)
            for i, target in enumerate(targets)
        ]
        base += len(targets)
        for copy in copies:
            copy.wait_recv()
        waits.extend(copies)
        total = source[...]
        for i in range(len(targets)):
            total = total + landing[i]
        return total

    g1[...] = exchange(g0, r_core, [core_peer])
    g2[...] = exchange(g1, r_x, [x_peer(k) for k in (1, 2, 3)])
    g3[...] = exchange(g2, r_y, [y_peer(k) for k in (1, 2, 3)])
    total = exchange(g3, r_z, [z_peer(k) for k in range(1, 8)])
    weights_ref[...] = weights_from(total)
    for copy in core_copies + x_copies + [z_copy] + waits:
        copy.wait_send()


def analysis(summed, observed, obs_var):
    vmem = pl.BlockSpec(memory_space=VMEM)
    piece = (2, 4 * MEMBERS, LANES)
    dma = pltpu.SemaphoreType.DMA
    return pl.pallas_call(
        analysis_kernel,
        out_shape=(
            jax.ShapeDtypeStruct((MEMBERS, 4 * LANES), F32),
            jax.ShapeDtypeStruct((4, LANES), F32),
            jax.ShapeDtypeStruct((MEMBERS, LANES), F32),
        ),
        in_specs=[pl.BlockSpec(memory_space=pl.ANY), vmem, vmem],
        out_specs=(vmem, vmem, vmem),
        scratch_shapes=[
            VMEM((4,) + piece, F32), VMEM((4,) + piece, F32), VMEM((3,) + piece, F32), VMEM(piece, F32), VMEM(piece[1:], F32),
        ]
        + [VMEM((MEMBERS, LANES), F32)] * 4
        + [VMEM((n, MEMBERS, LANES), F32) for n in (1, 3, 3, 7)]
        + [dma((4,)), dma((4,)), dma((4,)), dma((3,)), dma((3,)), dma, dma, dma((14,)), dma((14,))],
        compiler_params=pltpu.CompilerParams(collective_id=1, has_side_effects=True, vmem_limit_bytes=16 * 2**20),
        name="analysis",
    )(summed.reshape(4, 2, 2, 4 * MEMBERS, LANES), observed.reshape(4, LANES), obs_var.reshape(4, LANES))


LEVEL_STEP = 4


def update_kernel(weights_ref, forecast_ref, out_ref, high_ref, low_ref):
    @pl.when(pl.program_id(0) == 0)
    def _():
        size = MEMBERS * TILE_LAT
        tall = jnp.concatenate(
            [jnp.broadcast_to(weights_ref[b : b + 1, :], (TILE_LAT, LANES)) for b in range(MEMBERS)], axis=0
        )
        rows = lax.broadcasted_iota(jnp.int32, (LANES, size), 0)
        lanes = lax.broadcasted_iota(jnp.int32, (LANES, size), 1)
        spread = (lanes // TILE_LAT + 64 == rows).astype(F32)
        wide = jnp.dot(tall, spread, precision=lax.Precision.HIGHEST, preferred_element_type=F32)
        r = lax.broadcasted_iota(jnp.int32, (size, size), 0)
        c = lax.broadcasted_iota(jnp.int32, (size, size), 1)
        wide = jnp.where(lax.rem(r, TILE_LAT) == lax.rem(c, TILE_LAT), wide, 0.0)
        high = wide.astype(BF16)
        high_ref[...] = high
        low_ref[...] = (wide - high.astype(F32)).astype(BF16)

    for level in range(LEVEL_STEP):
        values = forecast_ref[:, level].reshape(MEMBERS * TILE_LAT, LANES)
        high = values.astype(BF16)
        low = (values - high.astype(F32)).astype(BF16)
        out = jnp.dot(high_ref[...], high, preferred_element_type=F32)
        out += jnp.dot(high_ref[...], low, preferred_element_type=F32)
        out += jnp.dot(low_ref[...], high, preferred_element_type=F32)
        out_ref[:, level] = out.reshape(MEMBERS, TILE_LAT, LANES)


def update(weights, forecast):
    size = MEMBERS * TILE_LAT
    block = pl.BlockSpec((MEMBERS, LEVEL_STEP, TILE_LAT, LANES), lambda i: (0, i, 0, 0))
    return pl.pallas_call(
        update_kernel,
        grid=(LEVELS // LEVEL_STEP,),
        out_shape=jax.ShapeDtypeStruct(forecast.shape, F32),
        in_specs=[pl.BlockSpec((MEMBERS, LANES), lambda i: (0, 0)), block],
        out_specs=block,
        scratch_shapes=[VMEM((size, size), BF16), VMEM((size, size), BF16)],
        compiler_params=pltpu.CompilerParams(vmem_limit_bytes=16 * 2**20),
        name="update",
    )(weights, forecast)


def per_device(
    sample_deviations, east_courant, north_courant, production, loss_rate,
    entry_count, entry_row, entry_block, path_weight, observed, obs_var,
):
    n = sample_deviations
    for repeat in range(2):
        lon_framed = extended(n, (("lon", 3),), 1, True)
        lat_framed = extended(n, (("lat", 2),), 1, False)
        n = advance(
            n, lon_framed[..., :-2], lon_framed[..., 2:], lat_framed[..., :-2, :], lat_framed[..., 2:, :],
            east_courant, north_courant, production, loss_rate,
        )
    content = (jnp.sum(n, axis=1) / math.sqrt(LEVELS)).astype(BF16)
    content = jnp.transpose(content, (1, 0, 2))
    summed = ray_sums(entry_count, entry_row, entry_block, content, path_weight)
    prior, innovation, weights = analysis(summed, observed, obs_var)
    return update(weights, n), prior, innovation.reshape(4 * LANES)


def solution(mesh):
    in_specs = (
        P(None, None, "lat", "lon"),
        P(None, "lat", "lon"),
        P(None, "lat", "lon"),
        P(None, "lat", "lon"),
        P(None, "lat", "lon"),
        P(("lon", "lat")),
        P(("lon", "lat")),
        P(("lon", "lat")),
        P(("lon", "lat"), None, None),
        P(("lon", "lat")),
        P(("lon", "lat")),
    )
    out_specs = (P(None, None, "lat", "lon"), P(None, ("lon", "lat")), P(("lon", "lat")))
    return jax.shard_map(per_device, mesh=mesh, in_specs=in_specs, out_specs=out_specs, check_vma=False)
```

```python
import math

import jax
import jax.numpy as jnp
from jax import lax
from jax.experimental import pallas as pl
from jax.experimental.pallas import tpu as pltpu
from jax.sharding import PartitionSpec as P

MEMBERS = 32
LEVELS = 32
TILE_LAT = 8
LANES = 128
SLOTS_TILE = 48
COL_BLOCKS = 64
MESH = pl.DeviceIdType.MESH
VMEM = pltpu.VMEM
F32 = jnp.float32
BF16 = jnp.bfloat16


CHUNKS = 8
CHUNK = LEVELS // CHUNKS
BATCH = 32
PAIRS = MEMBERS // 2


def forecast_kernel(
    east_ref, north_ref, source_ref, loss_ref, n_ref, out_ref, content_ref,
    coefs, own, beyond, result, edges, to_east, to_west, edges_west, edges_east, beyond_west, beyond_east,
    coef_edges, coef_west, coef_east, coef_beyond, frame0, frame_beyond, frame1, total,
    load_sem, coef_sem, store_sem, small_send, small_recv, up_send, up_recv, down_send, down_recv,
):
    lon, lat = lax.axis_index("lon"), lax.axis_index("lat")
    east, west = lax.rem(lon + 1, 16), lax.rem(lon + 15, 16)
    north, south = lax.rem(lat + 1, 16), lax.rem(lat + 15, 16)
    has_north, has_south = lat < 15, lat > 0
    coef_loads = [
        pltpu.make_async_copy(ref, coefs.at[i], coef_sem.at[i])
        for i, ref in enumerate((east_ref, north_ref, source_ref, loss_ref))
    ]
    for item in coef_loads:
        item.start()
    half = pl.ds(0, MEMBERS // 2), pl.ds(MEMBERS // 2, MEMBERS // 2)
    loads = [pltpu.make_async_copy(n_ref.at[part], own.at[part], load_sem.at[i]) for i, part in enumerate(half)]
    for item in loads:
        item.start()
    barrier = pltpu.get_barrier_semaphore()
    for peer in [(east, lat), (west, lat)] + [(i, j) for j in (north, south) for i in (lon, east, west)]:
        pl.semaphore_signal(barrier, inc=1, device_id=peer, device_id_type=MESH)


    def clear(part):
        size = part.size
        coef_beyond[:, :, part] = jnp.zeros((4, LEVELS, size, LANES), F32)
        beyond_west[:, part] = jnp.zeros((PAIRS, size, LANES), F32)
        beyond_east[:, part] = jnp.zeros((PAIRS, size, LANES), F32)

        @pl.loop(0, MEMBERS)
        def _(m):
            beyond[m, :, part] = jnp.zeros((LEVELS, size, LANES), F32)

    clear(pl.ds(2, TILE_LAT - 4))

    @pl.when(lat == 15)
    def _():
        clear(pl.ds(0, 2))

    @pl.when(lat == 0)
    def _():
        clear(pl.ds(TILE_LAT - 2, 2))

    lanes = lax.broadcasted_iota(jnp.int32, (TILE_LAT, LANES), 1)
    rows = lax.broadcasted_iota(jnp.int32, (TILE_LAT, LANES), 0)
    group, slot = lanes // 4, lax.rem(lanes, 4)
    is_first, is_last = rows == 0, rows == TILE_LAT - 1

    def packed(ref, part):
        out = jnp.zeros((ref[part, 0].shape[0], TILE_LAT, LANES), F32)
        for level in range(LEVELS):
            out = jnp.where(group == level, pltpu.roll(ref[part, level], (4 * level + 2) % LANES, 2), out)
        return out

    for item in coef_loads:
        item.wait()
    coef_edges[...] = packed(coefs, pl.ds(0, 4))
    for i, item in enumerate(loads):
        item.wait()
        edges[half[i]] = packed(own, half[i])
    first, second = edges[half[0]], edges[half[1]]
    to_east[...] = jnp.where(slot < 2, first, pltpu.roll(second, 2, 2))
    to_west[...] = jnp.where(slot >= 2, first, pltpu.roll(second, LANES - 2, 2))
    pl.semaphore_wait(barrier, 8)

    def copy(src, dst, send_sem, recv_sem, peer):
        return pltpu.make_async_remote_copy(
            src_ref=src, dst_ref=dst, send_sem=send_sem, recv_sem=recv_sem, device_id=peer, device_id_type=MESH
        )

    def small(i, src, dst, peer):
        return copy(src, dst, small_send.at[i], small_recv.at[i], peer)

    last, initial = pl.ds(TILE_LAT - 1, 1), pl.ds(0, 1)
    across = [
        small(0, coef_edges, coef_west, (east, lat)),
        small(1, coef_edges, coef_east, (west, lat)),
        small(2, to_east, edges_west, (east, lat)),
        small(3, to_west, edges_east, (west, lat)),
    ]
    up = [
        small(4, to_east.at[:, last], beyond_west.at[:, last], (east, north)),
        small(5, to_west.at[:, last], beyond_east.at[:, last], (west, north)),
        small(6, coefs.at[:, :, last], coef_beyond.at[:, :, last], (lon, north)),
    ]
    down = [
        small(7, to_east.at[:, initial], beyond_west.at[:, initial], (east, south)),
        small(8, to_west.at[:, initial], beyond_east.at[:, initial], (west, south)),
        small(9, coefs.at[:, :, initial], coef_beyond.at[:, :, initial], (lon, south)),
    ]

    def bulk_up(q):
        levels = pl.ds(q * CHUNK, CHUNK)
        part = pl.ds(TILE_LAT - 2, 2)
        return copy(n_ref.at[:, levels, part], beyond.at[:, levels, part], up_send.at[q], up_recv.at[q], (lon, north))

    def bulk_down(q):
        levels = pl.ds(q * CHUNK, CHUNK)
        part = pl.ds(0, 2)
        return copy(n_ref.at[:, levels, part], beyond.at[:, levels, part], down_send.at[q], down_recv.at[q], (lon, south))

    for item in across:
        item.start()

    @pl.when(has_north)
    def _():
        for item in up:
            item.start()

    @pl.when(has_south)
    def _():
        for item in down:
            item.start()

    for q in range(CHUNKS):

        @pl.when(has_north)
        def _():
            bulk_up(q).start()

        @pl.when(has_south)
        def _():
            bulk_down(q).start()

    for item in across:
        item.wait()

    @pl.when(has_south)
    def _():
        for item in up:
            item.wait_recv()

    @pl.when(has_north)
    def _():
        for item in down:
            item.wait_recv()

    def prepared(u, v, source, loss):
        keep = 1.0 - loss
        return keep * (1.0 - jnp.abs(u) - jnp.abs(v)), keep * jnp.abs(u), keep * jnp.abs(v), source, u > 0.0, v > 0.0

    def step(n, west_cell, east_cell, outside, prep):
        centre, along, across_, source, from_west, from_south = prep
        north_cell = pltpu.roll(jnp.where(is_first, outside, n), TILE_LAT - 1, 1)
        south_cell = pltpu.roll(jnp.where(is_last, outside, n), 1, 1)
        upwind_lon = jnp.where(from_west, west_cell, east_cell)
        upwind_lat = jnp.where(from_south, south_cell, north_cell)
        return centre * n + along * upwind_lon + across_ * upwind_lat + source

    def framed_step(n, frame, outside, prep):
        west_cell = pltpu.roll(jnp.where(lanes == LANES - 1, frame, n), 1, 2)
        east_cell = pltpu.roll(jnp.where(lanes == 0, frame, n), LANES - 1, 2)
        return step(n, west_cell, east_cell, outside, prep)

    edge_prep = prepared(*[jnp.where(slot == 1, coef_west[i], coef_east[i]) for i in range(4)])

    for i, part in enumerate(half):
        mine, from_west, from_east = edges[part], edges_west[...], edges_east[...]
        outside_west, outside_east = beyond_west[...], beyond_east[...]
        if i:
            from_west, outside_west = (pltpu.roll(v, LANES - 2, 2) for v in (from_west, outside_west))
            from_east, outside_east = (pltpu.roll(v, 2, 2) for v in (from_east, outside_east))
        frame = jnp.where(slot == 1, from_west, from_east)
        outside = jnp.where(slot == 1, outside_west, outside_east)
        west_cell = pltpu.roll(jnp.where(slot == 0, from_west, mine), 1, 2)
        east_cell = pltpu.roll(jnp.where(slot == 3, from_east, mine), LANES - 1, 2)
        frame0[part] = frame
        frame_beyond[part] = outside
        frame1[part] = step(frame, west_cell, east_cell, outside, edge_prep)
    total[...] = jnp.zeros_like(total)

    @pl.loop(0, CHUNKS)
    def _(q):
        @pl.when(has_south)
        def _():
            bulk_up(q).wait_recv()

        @pl.when(has_north)
        def _():
            bulk_down(q).wait_recv()

        @pl.loop(0, CHUNK)
        def _(i):
            level = q * CHUNK + i
            prep = prepared(*[coefs[k, level] for k in range(4)])
            prep_beyond = prepared(*[coef_beyond[k, level] for k in range(4)])
            shift = lax.rem(2 * LANES - 2 - 4 * level, LANES)

            @pl.loop(0, MEMBERS // BATCH)
            def _(g):
                part = pl.ds(g * BATCH, BATCH)
                n, out = own[part, level], beyond[part, level]
                n1 = framed_step(n, pltpu.roll(frame0[part], shift, 2), out, prep)
                out1 = framed_step(out, pltpu.roll(frame_beyond[part], shift, 2), n, prep_beyond)
                n2 = framed_step(n1, pltpu.roll(frame1[part], shift, 2), out1, prep)
                result[part, level] = n2
                total[part] += n2

        levels = pl.ds(q * CHUNK, CHUNK)
        pltpu.make_async_copy(result.at[:, levels], out_ref.at[:, levels], store_sem.at[q]).start()

    flat = total.reshape(MEMBERS * TILE_LAT, LANES)
    for y in range(TILE_LAT):
        content_ref[y] = (flat[pl.ds(y, MEMBERS, stride=TILE_LAT), :] / math.sqrt(LEVELS)).astype(BF16)

    @pl.when(has_north)
    def _():
        for item in up:
            item.wait_send()
        for q in range(CHUNKS):
            bulk_up(q).wait_send()

    @pl.when(has_south)
    def _():
        for item in down:
            item.wait_send()
        for q in range(CHUNKS):
            bulk_down(q).wait_send()

    for q in range(CHUNKS):
        levels = pl.ds(q * CHUNK, CHUNK)
        pltpu.make_async_copy(result.at[:, levels], out_ref.at[:, levels], store_sem.at[q]).wait()


def forecast(n, east_courant, north_courant, production, loss_rate):
    vmem = pl.BlockSpec(memory_space=VMEM)
    hbm = pl.BlockSpec(memory_space=pl.ANY)
    field = VMEM((MEMBERS, LEVELS, TILE_LAT, LANES), F32)
    packs = VMEM((MEMBERS, TILE_LAT, LANES), F32)
    pairs = VMEM((PAIRS, TILE_LAT, LANES), F32)
    coef_packs = VMEM((4, TILE_LAT, LANES), F32)
    dma = pltpu.SemaphoreType.DMA
    return pl.pallas_call(
        forecast_kernel,
        out_shape=(
            jax.ShapeDtypeStruct(n.shape, F32),
            jax.ShapeDtypeStruct((TILE_LAT, MEMBERS, LANES), BF16),
        ),
        in_specs=[hbm] * 5,
        out_specs=(hbm, vmem),
        scratch_shapes=[VMEM((4, LEVELS, TILE_LAT, LANES), F32)]
        + [field] * 3
        + [packs] + [pairs] * 6
        + [coef_packs] * 3
        + [VMEM((4, LEVELS, TILE_LAT, LANES), F32)]
        + [packs] * 4
        + [dma((2,)), dma((4,)), dma((CHUNKS,)), dma((10,)), dma((10,))]
        + [dma((CHUNKS,))] * 4,
        compiler_params=pltpu.CompilerParams(collective_id=2, has_side_effects=True, vmem_limit_bytes=60 * 2**20),
        name="forecast",
    )(east_courant, north_courant, production, loss_rate, n)


def ray_kernel(count_ref, row_ref, block_ref, content_ref, weight_ref, summed_ref, part_ref):
    summed_ref[...] = jnp.zeros_like(summed_ref)
    for k in range(SLOTS_TILE):
        picked = content_ref[row_ref[k]]
        part_ref[k] = jnp.dot(picked, weight_ref[k], preferred_element_type=F32)
    for k in range(SLOTS_TILE):
        block = block_ref[k]
        live = k < count_ref[0]
        summed_ref[block] += jnp.where(live, part_ref[k], 0.0)


def ray_sums(entry_count, entry_row, entry_block, content, path_weight):
    smem = pl.BlockSpec(memory_space=pltpu.SMEM)
    vmem = pl.BlockSpec(memory_space=VMEM)
    return pl.pallas_call(
        ray_kernel,
        out_shape=jax.ShapeDtypeStruct((COL_BLOCKS, MEMBERS, LANES), F32),
        in_specs=[smem, smem, smem, vmem, vmem],
        out_specs=vmem,
        scratch_shapes=[VMEM((SLOTS_TILE, MEMBERS, LANES), F32)],
        compiler_params=pltpu.CompilerParams(vmem_limit_bytes=16 * 2**20),
        name="ray_sums",
    )(entry_count, entry_row, entry_block, content, path_weight)


def weights_from(total):
    rows = lax.broadcasted_iota(jnp.int32, (MEMBERS, LANES), 0)
    lanes = lax.broadcasted_iota(jnp.int32, (MEMBERS, LANES), 1)
    inverse_lanes = (lanes >= 64) & (lanes < 64 + MEMBERS)
    work = total + jnp.where(lanes == rows, MEMBERS - 1.0, 0.0) + jnp.where(lanes == rows + 64, 1.0, 0.0)
    for j in range(MEMBERS):
        column = jnp.broadcast_to(work[:, j : j + 1], (MEMBERS, LANES))
        pivot = column[j : j + 1, :]
        scale = jnp.where(rows > j, column, 0.0) * (1.0 / pivot)
        work = work - scale * work[j : j + 1, :]
    diagonal = jnp.sum(jnp.where(lanes == rows, work, 0.0), axis=1, keepdims=True)
    work = work / jnp.sqrt(diagonal)
    inverse = jnp.where(inverse_lanes, work, 0.0)
    halfway = work[:, MEMBERS : MEMBERS + 1]
    mean_weights = jnp.sum(inverse * halfway, axis=0, keepdims=True)
    transform = jnp.where(inverse_lanes, mean_weights + math.sqrt(MEMBERS - 1.0) * inverse, 0.0)
    rest = (1.0 - jnp.sum(transform, axis=1, keepdims=True)) * (1.0 / MEMBERS)
    return jnp.where(inverse_lanes, transform + rest, 0.0)


def analysis_kernel(
    summed_ref, observed_ref, var_ref, prior_ref, innovation_ref, weights_ref,
    own, from_core, from_x, half, from_z, g0, g1, g2, g3, r_core, r_x, r_y, r_z,
    own_sem, core_send, core_recv, x_send, x_recv, z_send, z_recv, a_send, a_recv,
):
    lon, lat = lax.axis_index("lon"), lax.axis_index("lat")
    x, z_hi, core = lat // 4, lax.rem(lat // 2, 2), lax.rem(lat, 2)
    z_lo, y = lon // 4, lax.rem(lon, 4)

    def x_peer(k):
        return (lon, lax.rem(lat + 4 * k, 16))

    def y_peer(k):
        return (z_lo * 4 + lax.rem(y + k, 4), lat)

    def z_peer(k):
        z = lax.rem(z_hi * 4 + z_lo + k, 8)
        return (lax.rem(z, 4) * 4 + y, x * 4 + (z // 4) * 2 + core)

    core_peer = (lon, lat + 1 - 2 * core)
    peers = [core_peer] + [x_peer(k) for k in (1, 2, 3)] + [y_peer(k) for k in (1, 2, 3)]
    peers += [z_peer(k) for k in range(1, 8)]
    barrier = pltpu.get_barrier_semaphore()
    for peer in peers:
        pl.semaphore_signal(barrier, inc=1, device_id=peer, device_id_type=MESH)
    order = (2, 1, 3, 0)
    local = []
    for j in order:
        copy = pltpu.make_async_copy(summed_ref.at[lax.rem(x + j, 4), :, core], own.at[j], own_sem.at[j])
        copy.start()
        local.append(copy)
    pl.semaphore_wait(barrier, len(peers))

    def send(src, dst, send_sem, recv_sem, peer):
        copy = pltpu.make_async_remote_copy(
            src_ref=src, dst_ref=dst, send_sem=send_sem, recv_sem=recv_sem, device_id=peer, device_id_type=MESH
        )
        copy.start()
        return copy

    core_copies = [
        send(summed_ref.at[lax.rem(x + j, 4), :, 1 - core], from_core.at[j], core_send.at[j], core_recv.at[j], core_peer)
        for j in order
    ]
    x_copies = []
    for i, j in enumerate(order):
        local[i].wait()
        core_copies[i].wait_recv()
        own[j] = own[j] + from_core[j]
        if j:
            x_copies.append(send(own.at[j], from_x.at[j - 1], x_send.at[j - 1], x_recv.at[j - 1], x_peer(j)))
    for copy in x_copies:
        copy.wait_recv()
    half[...] = own[0] + from_x[0] + from_x[1] + from_x[2]
    z_copy = send(half.at[1 - z_hi], from_z, z_send, z_recv, z_peer(4))
    z_copy.wait_recv()
    samples = half[z_hi] + from_z[...]

    spreads, scaled = [], []
    for b in range(4):
        block = samples[b * MEMBERS : (b + 1) * MEMBERS]
        prior_ref[:, b * LANES : (b + 1) * LANES] = block
        mean = jnp.sum(block, axis=0, keepdims=True) * (1.0 / MEMBERS)
        misfit = observed_ref[b : b + 1, :] - mean
        variance = var_ref[b : b + 1, :]
        innovation_ref[b : b + 1, :] = misfit / jnp.sqrt(variance)
        spread = block - mean
        spreads.append(jnp.concatenate([spread, jnp.broadcast_to(misfit, (MEMBERS, LANES)), jnp.zeros((64, LANES), F32)], axis=0))
        scaled.append(spread / variance)
    gram = lax.dot_general(
        jnp.concatenate(scaled, axis=1), jnp.concatenate(spreads, axis=1), (((1,), (1,)), ((), ())),
        precision=lax.Precision.HIGHEST, preferred_element_type=F32,
    )
    lanes = lax.broadcasted_iota(jnp.int32, (MEMBERS, LANES), 1)
    g0[...] = jnp.where(lanes <= MEMBERS, gram, 0.0)

    waits = []
    base = 0

    def exchange(source, landing, targets):
        nonlocal base
        copies = [
            send(source, landing.at[i], a_send.at[base + i], a_recv.at[base + i], target)
            for i, target in enumerate(targets)
        ]
        base += len(targets)
        for copy in copies:
            copy.wait_recv()
        waits.extend(copies)
        total = source[...]
        for i in range(len(targets)):
            total = total + landing[i]
        return total

    g1[...] = exchange(g0, r_core, [core_peer])
    g2[...] = exchange(g1, r_x, [x_peer(k) for k in (1, 2, 3)])
    g3[...] = exchange(g2, r_y, [y_peer(k) for k in (1, 2, 3)])
    total = exchange(g3, r_z, [z_peer(k) for k in range(1, 8)])
    weights_ref[...] = weights_from(total)
    for copy in core_copies + x_copies + [z_copy] + waits:
        copy.wait_send()


def analysis(summed, observed, obs_var):
    vmem = pl.BlockSpec(memory_space=VMEM)
    piece = (2, 4 * MEMBERS, LANES)
    dma = pltpu.SemaphoreType.DMA
    return pl.pallas_call(
        analysis_kernel,
        out_shape=(
            jax.ShapeDtypeStruct((MEMBERS, 4 * LANES), F32),
            jax.ShapeDtypeStruct((4, LANES), F32),
            jax.ShapeDtypeStruct((MEMBERS, LANES), F32),
        ),
        in_specs=[pl.BlockSpec(memory_space=pl.ANY), vmem, vmem],
        out_specs=(vmem, vmem, vmem),
        scratch_shapes=[
            VMEM((4,) + piece, F32), VMEM((4,) + piece, F32), VMEM((3,) + piece, F32), VMEM(piece, F32), VMEM(piece[1:], F32),
        ]
        + [VMEM((MEMBERS, LANES), F32)] * 4
        + [VMEM((n, MEMBERS, LANES), F32) for n in (1, 3, 3, 7)]
        + [dma((4,)), dma((4,)), dma((4,)), dma((3,)), dma((3,)), dma, dma, dma((14,)), dma((14,))],
        compiler_params=pltpu.CompilerParams(collective_id=1, has_side_effects=True, vmem_limit_bytes=16 * 2**20),
        name="analysis",
    )(summed.reshape(4, 2, 2, 4 * MEMBERS, LANES), observed.reshape(4, LANES), obs_var.reshape(4, LANES))


LEVEL_STEP = 4


def update_kernel(weights_ref, forecast_ref, out_ref, high_ref, low_ref):
    @pl.when(pl.program_id(0) == 0)
    def _():
        size = MEMBERS * TILE_LAT
        tall = jnp.concatenate(
            [jnp.broadcast_to(weights_ref[b : b + 1, :], (TILE_LAT, LANES)) for b in range(MEMBERS)], axis=0
        )
        rows = lax.broadcasted_iota(jnp.int32, (LANES, size), 0)
        lanes = lax.broadcasted_iota(jnp.int32, (LANES, size), 1)
        spread = (lanes // TILE_LAT + 64 == rows).astype(F32)
        wide = jnp.dot(tall, spread, precision=lax.Precision.HIGHEST, preferred_element_type=F32)
        r = lax.broadcasted_iota(jnp.int32, (size, size), 0)
        c = lax.broadcasted_iota(jnp.int32, (size, size), 1)
        wide = jnp.where(lax.rem(r, TILE_LAT) == lax.rem(c, TILE_LAT), wide, 0.0)
        high = wide.astype(BF16)
        high_ref[...] = high
        low_ref[...] = (wide - high.astype(F32)).astype(BF16)

    for level in range(LEVEL_STEP):
        values = forecast_ref[:, level].reshape(MEMBERS * TILE_LAT, LANES)
        high = values.astype(BF16)
        low = (values - high.astype(F32)).astype(BF16)
        out = jnp.dot(high_ref[...], high, preferred_element_type=F32)
        out += jnp.dot(high_ref[...], low, preferred_element_type=F32)
        out += jnp.dot(low_ref[...], high, preferred_element_type=F32)
        out_ref[:, level] = out.reshape(MEMBERS, TILE_LAT, LANES)


def update(weights, forecast):
    size = MEMBERS * TILE_LAT
    block = pl.BlockSpec((MEMBERS, LEVEL_STEP, TILE_LAT, LANES), lambda i: (0, i, 0, 0))
    return pl.pallas_call(
        update_kernel,
        grid=(LEVELS // LEVEL_STEP,),
        out_shape=jax.ShapeDtypeStruct(forecast.shape, F32),
        in_specs=[pl.BlockSpec((MEMBERS, LANES), lambda i: (0, 0)), block],
        out_specs=block,
        scratch_shapes=[VMEM((size, size), BF16), VMEM((size, size), BF16)],
        compiler_params=pltpu.CompilerParams(vmem_limit_bytes=16 * 2**20),
        name="update",
    )(weights, forecast)


def per_device(
    sample_deviations, east_courant, north_courant, production, loss_rate,
    entry_count, entry_row, entry_block, path_weight, observed, obs_var,
):
    n, content = forecast(sample_deviations, east_courant, north_courant, production, loss_rate)
    summed = ray_sums(entry_count, entry_row, entry_block, content, path_weight)
    prior, innovation, weights = analysis(summed, observed, obs_var)
    return update(weights, n), prior, innovation.reshape(4 * LANES)


def solution(mesh):
    in_specs = (
        P(None, None, "lat", "lon"),
        P(None, "lat", "lon"),
        P(None, "lat", "lon"),
        P(None, "lat", "lon"),
        P(None, "lat", "lon"),
        P(("lon", "lat")),
        P(("lon", "lat")),
        P(("lon", "lat")),
        P(("lon", "lat"), None, None),
        P(("lon", "lat")),
        P(("lon", "lat")),
    )
    out_specs = (P(None, None, "lat", "lon"), P(None, ("lon", "lat")), P(("lon", "lat")))
    return jax.shard_map(per_device, mesh=mesh, in_specs=in_specs, out_specs=out_specs, check_vma=False)
```

```python
import math

import jax
import jax.numpy as jnp
from jax import lax
from jax.experimental import pallas as pl
from jax.experimental.pallas import tpu as pltpu
from jax.sharding import PartitionSpec as P

MEMBERS = 32
LEVELS = 32
TILE_LAT = 8
LANES = 128
SLOTS_TILE = 48
COL_BLOCKS = 64
MESH = pl.DeviceIdType.MESH
VMEM = pltpu.VMEM
F32 = jnp.float32
BF16 = jnp.bfloat16


CHUNKS = 8
CHUNK = LEVELS // CHUNKS
BATCH = 32
PAIRS = MEMBERS // 2


def forecast_kernel(
    coefs, n_ref, out_ref, content_ref,
    own, beyond, edges, to_east, to_west, edges_west, edges_east, beyond_west, beyond_east,
    coef_edges, coef_west, coef_east, coef_beyond, frame0, frame_beyond, frame1, total,
    load_sem, small_send, small_recv, up_send, up_recv, down_send, down_recv,
):
    lon, lat = lax.axis_index("lon"), lax.axis_index("lat")
    east, west = lax.rem(lon + 1, 16), lax.rem(lon + 15, 16)
    north, south = lax.rem(lat + 1, 16), lax.rem(lat + 15, 16)
    has_north, has_south = lat < 15, lat > 0
    half = pl.ds(0, MEMBERS // 2), pl.ds(MEMBERS // 2, MEMBERS // 2)
    loads = [pltpu.make_async_copy(n_ref.at[part], own.at[part], load_sem.at[i]) for i, part in enumerate(half)]
    for item in loads:
        item.start()
    barrier = pltpu.get_barrier_semaphore()
    for peer in [(east, lat), (west, lat)] + [(i, j) for j in (north, south) for i in (lon, east, west)]:
        pl.semaphore_signal(barrier, inc=1, device_id=peer, device_id_type=MESH)


    def clear(part):
        size = part.size
        coef_beyond[:, :, part] = jnp.zeros((4, LEVELS, size, LANES), F32)
        beyond_west[:, part] = jnp.zeros((PAIRS, size, LANES), F32)
        beyond_east[:, part] = jnp.zeros((PAIRS, size, LANES), F32)

        @pl.loop(0, MEMBERS)
        def _(m):
            beyond[m, :, part] = jnp.zeros((LEVELS, size, LANES), F32)

    clear(pl.ds(2, TILE_LAT - 4))

    @pl.when(lat == 15)
    def _():
        clear(pl.ds(0, 2))

    @pl.when(lat == 0)
    def _():
        clear(pl.ds(TILE_LAT - 2, 2))

    lanes = lax.broadcasted_iota(jnp.int32, (TILE_LAT, LANES), 1)
    rows = lax.broadcasted_iota(jnp.int32, (TILE_LAT, LANES), 0)
    group, slot = lanes // 4, lax.rem(lanes, 4)
    is_first, is_last = rows == 0, rows == TILE_LAT - 1

    def packed(ref, part):
        out = jnp.zeros((ref[part, 0].shape[0], TILE_LAT, LANES), F32)
        for level in range(LEVELS):
            out = jnp.where(group == level, pltpu.roll(ref[part, level], (4 * level + 2) % LANES, 2), out)
        return out

    coef_edges[...] = packed(coefs, pl.ds(0, 4))
    for i, item in enumerate(loads):
        item.wait()
        edges[half[i]] = packed(own, half[i])
    first, second = edges[half[0]], edges[half[1]]
    to_east[...] = jnp.where(slot < 2, first, pltpu.roll(second, 2, 2))
    to_west[...] = jnp.where(slot >= 2, first, pltpu.roll(second, LANES - 2, 2))
    pl.semaphore_wait(barrier, 8)

    def copy(src, dst, send_sem, recv_sem, peer):
        return pltpu.make_async_remote_copy(
            src_ref=src, dst_ref=dst, send_sem=send_sem, recv_sem=recv_sem, device_id=peer, device_id_type=MESH
        )

    def small(i, src, dst, peer):
        return copy(src, dst, small_send.at[i], small_recv.at[i], peer)

    last, initial = pl.ds(TILE_LAT - 1, 1), pl.ds(0, 1)
    across = [
        small(0, coef_edges, coef_west, (east, lat)),
        small(1, coef_edges, coef_east, (west, lat)),
        small(2, to_east, edges_west, (east, lat)),
        small(3, to_west, edges_east, (west, lat)),
    ]
    up = [
        small(4, to_east.at[:, last], beyond_west.at[:, last], (east, north)),
        small(5, to_west.at[:, last], beyond_east.at[:, last], (west, north)),
        small(6, coefs.at[:, :, last], coef_beyond.at[:, :, last], (lon, north)),
    ]
    down = [
        small(7, to_east.at[:, initial], beyond_west.at[:, initial], (east, south)),
        small(8, to_west.at[:, initial], beyond_east.at[:, initial], (west, south)),
        small(9, coefs.at[:, :, initial], coef_beyond.at[:, :, initial], (lon, south)),
    ]

    def bulk_up(q):
        levels = pl.ds(q * CHUNK, CHUNK)
        part = pl.ds(TILE_LAT - 2, 2)
        return copy(n_ref.at[:, levels, part], beyond.at[:, levels, part], up_send.at[q], up_recv.at[q], (lon, north))

    def bulk_down(q):
        levels = pl.ds(q * CHUNK, CHUNK)
        part = pl.ds(0, 2)
        return copy(n_ref.at[:, levels, part], beyond.at[:, levels, part], down_send.at[q], down_recv.at[q], (lon, south))

    for item in across:
        item.start()

    @pl.when(has_north)
    def _():
        for item in up:
            item.start()

    @pl.when(has_south)
    def _():
        for item in down:
            item.start()

    for q in range(CHUNKS):

        @pl.when(has_north)
        def _():
            bulk_up(q).start()

        @pl.when(has_south)
        def _():
            bulk_down(q).start()

    for item in across:
        item.wait()

    @pl.when(has_south)
    def _():
        for item in up:
            item.wait_recv()

    @pl.when(has_north)
    def _():
        for item in down:
            item.wait_recv()

    def prepared(u, v, source, loss):
        keep = 1.0 - loss
        return keep * (1.0 - jnp.abs(u) - jnp.abs(v)), keep * jnp.abs(u), keep * jnp.abs(v), source, u > 0.0, v > 0.0

    def step(n, west_cell, east_cell, outside, prep):
        centre, along, across_, source, from_west, from_south = prep
        north_cell = pltpu.roll(jnp.where(is_first, outside, n), TILE_LAT - 1, 1)
        south_cell = pltpu.roll(jnp.where(is_last, outside, n), 1, 1)
        upwind_lon = jnp.where(from_west, west_cell, east_cell)
        upwind_lat = jnp.where(from_south, south_cell, north_cell)
        return centre * n + along * upwind_lon + across_ * upwind_lat + source

    def framed_step(n, frame, outside, prep):
        west_cell = pltpu.roll(jnp.where(lanes == LANES - 1, frame, n), 1, 2)
        east_cell = pltpu.roll(jnp.where(lanes == 0, frame, n), LANES - 1, 2)
        return step(n, west_cell, east_cell, outside, prep)

    edge_prep = prepared(*[jnp.where(slot == 1, coef_west[i], coef_east[i]) for i in range(4)])

    for i, part in enumerate(half):
        mine, from_west, from_east = edges[part], edges_west[...], edges_east[...]
        outside_west, outside_east = beyond_west[...], beyond_east[...]
        if i:
            from_west, outside_west = (pltpu.roll(v, LANES - 2, 2) for v in (from_west, outside_west))
            from_east, outside_east = (pltpu.roll(v, 2, 2) for v in (from_east, outside_east))
        frame = jnp.where(slot == 1, from_west, from_east)
        outside = jnp.where(slot == 1, outside_west, outside_east)
        west_cell = pltpu.roll(jnp.where(slot == 0, from_west, mine), 1, 2)
        east_cell = pltpu.roll(jnp.where(slot == 3, from_east, mine), LANES - 1, 2)
        frame0[part] = frame
        frame_beyond[part] = outside
        frame1[part] = step(frame, west_cell, east_cell, outside, edge_prep)
    total[...] = jnp.zeros_like(total)

    @pl.loop(0, CHUNKS)
    def _(q):
        @pl.when(has_south)
        def _():
            bulk_up(q).wait_recv()

        @pl.when(has_north)
        def _():
            bulk_down(q).wait_recv()

        @pl.loop(0, CHUNK)
        def _(i):
            level = q * CHUNK + i
            prep = prepared(*[coefs[k, level] for k in range(4)])
            prep_beyond = prepared(*[coef_beyond[k, level] for k in range(4)])
            shift = lax.rem(2 * LANES - 2 - 4 * level, LANES)

            @pl.loop(0, MEMBERS // BATCH)
            def _(g):
                part = pl.ds(g * BATCH, BATCH)
                n, out = own[part, level], beyond[part, level]
                n1 = framed_step(n, pltpu.roll(frame0[part], shift, 2), out, prep)
                out1 = framed_step(out, pltpu.roll(frame_beyond[part], shift, 2), n, prep_beyond)
                n2 = framed_step(n1, pltpu.roll(frame1[part], shift, 2), out1, prep)
                out_ref[part, level] = n2
                total[part] += n2

    flat = total.reshape(MEMBERS * TILE_LAT, LANES)
    for y in range(TILE_LAT):
        content_ref[y] = (flat[pl.ds(y, MEMBERS, stride=TILE_LAT), :] / math.sqrt(LEVELS)).astype(BF16)

    @pl.when(has_north)
    def _():
        for item in up:
            item.wait_send()
        for q in range(CHUNKS):
            bulk_up(q).wait_send()

    @pl.when(has_south)
    def _():
        for item in down:
            item.wait_send()
        for q in range(CHUNKS):
            bulk_down(q).wait_send()


def forecast(n, east_courant, north_courant, production, loss_rate):
    vmem = pl.BlockSpec(memory_space=VMEM)
    hbm = pl.BlockSpec(memory_space=pltpu.HBM)
    field = VMEM((MEMBERS, LEVELS, TILE_LAT, LANES), F32)
    packs = VMEM((MEMBERS, TILE_LAT, LANES), F32)
    pairs = VMEM((PAIRS, TILE_LAT, LANES), F32)
    coef_packs = VMEM((4, TILE_LAT, LANES), F32)
    dma = pltpu.SemaphoreType.DMA
    return pl.pallas_call(
        forecast_kernel,
        out_shape=(
            jax.ShapeDtypeStruct(n.shape, F32),
            jax.ShapeDtypeStruct((TILE_LAT, MEMBERS, LANES), BF16),
        ),
        in_specs=[vmem, hbm],
        out_specs=(vmem, vmem),
        scratch_shapes=[field] * 2
        + [packs] + [pairs] * 6
        + [coef_packs] * 3
        + [VMEM((4, LEVELS, TILE_LAT, LANES), F32)]
        + [packs] * 4
        + [dma((2,)), dma((10,)), dma((10,))]
        + [dma((CHUNKS,))] * 4,
        compiler_params=pltpu.CompilerParams(collective_id=2, has_side_effects=True, vmem_limit_bytes=46 * 2**20),
        name="forecast",
    )(jnp.stack([east_courant, north_courant, production, loss_rate]), n)


def ray_kernel(count_ref, row_ref, block_ref, content_ref, weight_ref, summed_ref, part_ref):
    summed_ref[...] = jnp.zeros_like(summed_ref)
    for k in range(SLOTS_TILE):
        picked = content_ref[row_ref[k]]
        part_ref[k] = jnp.dot(picked, weight_ref[k], preferred_element_type=F32)
    for k in range(SLOTS_TILE):
        block = block_ref[k]
        live = k < count_ref[0]
        summed_ref[block] += jnp.where(live, part_ref[k], 0.0)


def ray_sums(entry_count, entry_row, entry_block, content, path_weight):
    smem = pl.BlockSpec(memory_space=pltpu.SMEM)
    vmem = pl.BlockSpec(memory_space=VMEM)
    return pl.pallas_call(
        ray_kernel,
        out_shape=jax.ShapeDtypeStruct((COL_BLOCKS, MEMBERS, LANES), F32),
        in_specs=[smem, smem, smem, vmem, vmem],
        out_specs=vmem,
        scratch_shapes=[VMEM((SLOTS_TILE, MEMBERS, LANES), F32)],
        compiler_params=pltpu.CompilerParams(vmem_limit_bytes=16 * 2**20),
        name="ray_sums",
    )(entry_count, entry_row, entry_block, content, path_weight)


def weights_from(total):
    rows = lax.broadcasted_iota(jnp.int32, (MEMBERS, LANES), 0)
    lanes = lax.broadcasted_iota(jnp.int32, (MEMBERS, LANES), 1)
    inverse_lanes = (lanes >= 64) & (lanes < 64 + MEMBERS)
    square = jnp.concatenate(
        [pltpu.roll(total[0:8], LANES - MEMBERS * k, 1) if k else total[0:8] for k in range(4)], axis=0
    )
    square = jnp.where(lanes < MEMBERS, square, 0.0)
    pull = jnp.sum(jnp.where(lanes == rows, total[8:9], 0.0), axis=1, keepdims=True)
    work = square + jnp.where(lanes == MEMBERS, pull, 0.0)
    work = work + jnp.where(lanes == rows, MEMBERS - 1.0, 0.0) + jnp.where(lanes == rows + 64, 1.0, 0.0)
    for j in range(MEMBERS):
        column = jnp.broadcast_to(work[:, j : j + 1], (MEMBERS, LANES))
        pivot = column[j : j + 1, :]
        scale = jnp.where(rows > j, column, 0.0) * (1.0 / pivot)
        work = work - scale * work[j : j + 1, :]
    diagonal = jnp.sum(jnp.where(lanes == rows, work, 0.0), axis=1, keepdims=True)
    work = work / jnp.sqrt(diagonal)
    inverse = jnp.where(inverse_lanes, work, 0.0)
    halfway = work[:, MEMBERS : MEMBERS + 1]
    mean_weights = jnp.sum(inverse * halfway, axis=0, keepdims=True)
    transform = jnp.where(inverse_lanes, mean_weights + math.sqrt(MEMBERS - 1.0) * inverse, 0.0)
    rest = (1.0 - jnp.sum(transform, axis=1, keepdims=True)) * (1.0 / MEMBERS)
    return jnp.where(inverse_lanes, transform + rest, 0.0)


def analysis_kernel(
    summed_ref, observed_ref, var_ref, prior_ref, innovation_ref, weights_ref,
    own, from_core, from_x, half, from_z, g0, g1, g2, r_plane, r_y, r_z,
    own_sem, core_send, core_recv, x_send, x_recv, z_send, z_recv, a_send, a_recv,
):
    lon, lat = lax.axis_index("lon"), lax.axis_index("lat")
    x, z_hi, core = lat // 4, lax.rem(lat // 2, 2), lax.rem(lat, 2)
    z_lo, y = lon // 4, lax.rem(lon, 4)

    def x_peer(k):
        return (lon, lax.rem(lat + 4 * k, 16))

    def y_peer(k):
        return (z_lo * 4 + lax.rem(y + k, 4), lat)

    def z_peer(k):
        z = lax.rem(z_hi * 4 + z_lo + k, 8)
        return (lax.rem(z, 4) * 4 + y, x * 4 + (z // 4) * 2 + core)

    core_peer = (lon, lat + 1 - 2 * core)
    across = lat + 1 - 2 * core
    plane_peers = [core_peer] + [x_peer(k) for k in (1, 2, 3)]
    plane_peers += [(lon, lax.rem(across + 4 * k, 16)) for k in (1, 2, 3)]
    peers = plane_peers + [y_peer(k) for k in (1, 2, 3)]
    peers += [z_peer(k) for k in range(1, 8)]
    barrier = pltpu.get_barrier_semaphore()
    for peer in peers:
        pl.semaphore_signal(barrier, inc=1, device_id=peer, device_id_type=MESH)
    order = (2, 1, 3, 0)
    local = []
    for j in order:
        copy = pltpu.make_async_copy(summed_ref.at[lax.rem(x + j, 4), :, core], own.at[j], own_sem.at[j])
        copy.start()
        local.append(copy)
    pl.semaphore_wait(barrier, len(peers))

    def send(src, dst, send_sem, recv_sem, peer):
        copy = pltpu.make_async_remote_copy(
            src_ref=src, dst_ref=dst, send_sem=send_sem, recv_sem=recv_sem, device_id=peer, device_id_type=MESH
        )
        copy.start()
        return copy

    core_copies = [
        send(summed_ref.at[lax.rem(x + j, 4), :, 1 - core], from_core.at[j], core_send.at[j], core_recv.at[j], core_peer)
        for j in order
    ]
    x_copies = []
    for i, j in enumerate(order):
        local[i].wait()
        core_copies[i].wait_recv()
        own[j] = own[j] + from_core[j]
        if j:
            x_copies.append(send(own.at[j], from_x.at[j - 1], x_send.at[j - 1], x_recv.at[j - 1], x_peer(j)))
    for copy in x_copies:
        copy.wait_recv()
    half[...] = own[0] + from_x[0] + from_x[1] + from_x[2]
    z_copy = send(half.at[1 - z_hi], from_z, z_send, z_recv, z_peer(4))
    z_copy.wait_recv()
    samples = half[z_hi] + from_z[...]

    spreads, scaled = [], []
    for b in range(4):
        block = samples[b * MEMBERS : (b + 1) * MEMBERS]
        prior_ref[:, b * LANES : (b + 1) * LANES] = block
        mean = jnp.sum(block, axis=0, keepdims=True) * (1.0 / MEMBERS)
        misfit = observed_ref[b : b + 1, :] - mean
        variance = var_ref[b : b + 1, :]
        innovation_ref[b : b + 1, :] = misfit / jnp.sqrt(variance)
        spread = block - mean
        spreads.append(jnp.concatenate([spread, jnp.zeros((LANES - MEMBERS, LANES), F32)], axis=0))
        scaled.append(jnp.concatenate([spread, jnp.broadcast_to(misfit, (8, LANES))], axis=0) / variance)
    gram = lax.dot_general(
        jnp.concatenate(scaled, axis=1), jnp.concatenate(spreads, axis=1), (((1,), (1,)), ((), ())),
        precision=lax.Precision.HIGHEST, preferred_element_type=F32,
    )
    lanes = lax.broadcasted_iota(jnp.int32, gram.shape, 1)
    square = jnp.where(lanes < MEMBERS, gram, 0.0)
    g0[0:8] = sum(
        pltpu.roll(square[8 * k : 8 * k + 8], MEMBERS * k, 1) if k else square[0:8] for k in range(4)
    )
    g0[8:9] = gram[MEMBERS : MEMBERS + 1]

    waits = []
    base = 0

    def exchange(source, landing, targets):
        nonlocal base
        copies = [
            send(source, landing.at[i], a_send.at[base + i], a_recv.at[base + i], target)
            for i, target in enumerate(targets)
        ]
        base += len(targets)
        for copy in copies:
            copy.wait_recv()
        waits.extend(copies)
        total = source[...]
        for i in range(len(targets)):
            total = total + landing[i]
        return total

    g1[...] = exchange(g0, r_plane, plane_peers)
    g2[...] = exchange(g1, r_y, [y_peer(k) for k in (1, 2, 3)])
    total = exchange(g2, r_z, [z_peer(k) for k in range(1, 8)])
    weights_ref[...] = weights_from(total)
    for copy in core_copies + x_copies + [z_copy] + waits:
        copy.wait_send()


def analysis(summed, observed, obs_var):
    vmem = pl.BlockSpec(memory_space=VMEM)
    piece = (2, 4 * MEMBERS, LANES)
    dma = pltpu.SemaphoreType.DMA
    return pl.pallas_call(
        analysis_kernel,
        out_shape=(
            jax.ShapeDtypeStruct((MEMBERS, 4 * LANES), F32),
            jax.ShapeDtypeStruct((4, LANES), F32),
            jax.ShapeDtypeStruct((MEMBERS, LANES), F32),
        ),
        in_specs=[pl.BlockSpec(memory_space=pl.ANY), vmem, vmem],
        out_specs=(vmem, vmem, vmem),
        scratch_shapes=[
            VMEM((4,) + piece, F32), VMEM((4,) + piece, F32), VMEM((3,) + piece, F32), VMEM(piece, F32), VMEM(piece[1:], F32),
        ]
        + [VMEM((9, LANES), F32)] * 3
        + [VMEM((n, 9, LANES), F32) for n in (7, 3, 7)]
        + [dma((4,)), dma((4,)), dma((4,)), dma((3,)), dma((3,)), dma, dma, dma((17,)), dma((17,))],
        compiler_params=pltpu.CompilerParams(collective_id=1, has_side_effects=True, vmem_limit_bytes=16 * 2**20),
        name="analysis",
    )(summed.reshape(4, 2, 2, 4 * MEMBERS, LANES), observed.reshape(4, LANES), obs_var.reshape(4, LANES))


PART = 8
PARTS = LEVELS // PART


def update_kernel(
    weights_ref, prior_ref, innovation_ref, forecast_ref, out_ref, prior_out, innovation_out,
    high_ref, low_ref, updated_ref, store_sem,
):
    def store(i):
        levels = pl.ds(i * PART, PART)
        return pltpu.make_async_copy(updated_ref.at[:, levels], out_ref.at[:, levels], store_sem.at[i])

    prior_out[...] = prior_ref[...]
    innovation_out[...] = innovation_ref[...]
    size = MEMBERS * TILE_LAT
    tall = jnp.concatenate(
        [jnp.broadcast_to(weights_ref[b : b + 1, :], (TILE_LAT, LANES)) for b in range(MEMBERS)], axis=0
    )
    rows = lax.broadcasted_iota(jnp.int32, (LANES, size), 0)
    lanes = lax.broadcasted_iota(jnp.int32, (LANES, size), 1)
    spread = (lanes // TILE_LAT + 64 == rows).astype(BF16)
    r = lax.broadcasted_iota(jnp.int32, (size, size), 0)
    c = lax.broadcasted_iota(jnp.int32, (size, size), 1)
    same = lax.rem(r, TILE_LAT) == lax.rem(c, TILE_LAT)
    high = tall.astype(BF16)
    low = (tall - high.astype(F32)).astype(BF16)
    for part, ref in ((high, high_ref), (low, low_ref)):
        wide = jnp.dot(part, spread, preferred_element_type=F32)
        ref[...] = jnp.where(same, wide, 0.0).astype(BF16)

    for step in range(PARTS):
        for level in range(step * PART, (step + 1) * PART, 2):
            values = jnp.concatenate(
                [forecast_ref[:, level + i].reshape(MEMBERS * TILE_LAT, LANES) for i in range(2)], axis=1
            )
            high = values.astype(BF16)
            low = (values - high.astype(F32)).astype(BF16)
            out = jnp.dot(high_ref[...], high, preferred_element_type=F32)
            out += jnp.dot(high_ref[...], low, preferred_element_type=F32)
            out += jnp.dot(low_ref[...], high, preferred_element_type=F32)
            for i in range(2):
                updated_ref[:, level + i] = out[:, i * LANES : (i + 1) * LANES].reshape(MEMBERS, TILE_LAT, LANES)

        store(step).start()
    for i in range(PARTS):
        store(i).wait()


def update(weights, prior, innovation, forecast):
    size = MEMBERS * TILE_LAT
    vmem = pl.BlockSpec(memory_space=VMEM)
    hbm = pl.BlockSpec(memory_space=pltpu.HBM)
    field = VMEM(forecast.shape, F32)
    dma = pltpu.SemaphoreType.DMA
    return pl.pallas_call(
        update_kernel,
        out_shape=tuple(jax.ShapeDtypeStruct(v.shape, F32) for v in (forecast, prior, innovation)),
        in_specs=[vmem] * 4,
        out_specs=(hbm, vmem, vmem),
        scratch_shapes=[VMEM((size, size), BF16)] * 2 + [field, dma((PARTS,))],
        compiler_params=pltpu.CompilerParams(vmem_limit_bytes=24 * 2**20),
        name="update",
    )(weights, prior, innovation, forecast)


def per_device(
    sample_deviations, east_courant, north_courant, production, loss_rate,
    entry_count, entry_row, entry_block, path_weight, observed, obs_var,
):
    n, content = forecast(sample_deviations, east_courant, north_courant, production, loss_rate)
    summed = ray_sums(entry_count, entry_row, entry_block, content, path_weight)
    prior, innovation, weights = analysis(summed, observed, obs_var)
    updated, prior, innovation = update(weights, prior, innovation, n)
    return updated, prior, innovation.reshape(4 * LANES)


def solution(mesh):
    in_specs = (
        P(None, None, "lat", "lon"),
        P(None, "lat", "lon"),
        P(None, "lat", "lon"),
        P(None, "lat", "lon"),
        P(None, "lat", "lon"),
        P(("lon", "lat")),
        P(("lon", "lat")),
        P(("lon", "lat")),
        P(("lon", "lat"), None, None),
        P(("lon", "lat")),
        P(("lon", "lat")),
    )
    out_specs = (P(None, None, "lat", "lon"), P(None, ("lon", "lat")), P(("lon", "lat")))
    return jax.shard_map(per_device, mesh=mesh, in_specs=in_specs, out_specs=out_specs, check_vma=False)
```

```python
import math

import jax
import jax.numpy as jnp
from jax import lax
from jax.experimental import pallas as pl
from jax.experimental.pallas import tpu as pltpu
from jax.sharding import PartitionSpec as P

MEMBERS = 32
LEVELS = 32
TILE_LAT = 8
LANES = 128
SLOTS_TILE = 48
COL_BLOCKS = 64
MESH = pl.DeviceIdType.MESH
VMEM = pltpu.VMEM
F32 = jnp.float32
BF16 = jnp.bfloat16


CHUNKS = 8
CHUNK = LEVELS // CHUNKS
BATCH = 32
PAIRS = MEMBERS // 2


def forecast_kernel(
    coefs, n_ref, out_ref, content_ref,
    own, beyond, edges, to_east, to_west, edges_west, edges_east, beyond_west, beyond_east,
    coef_edges, coef_west, coef_east, coef_beyond, frame0, frame_beyond, frame1, total,
    load_sem, small_send, small_recv, up_send, up_recv, down_send, down_recv,
):
    lon, lat = lax.axis_index("lon"), lax.axis_index("lat")
    east, west = lax.rem(lon + 1, 16), lax.rem(lon + 15, 16)
    north, south = lax.rem(lat + 1, 16), lax.rem(lat + 15, 16)
    has_north, has_south = lat < 15, lat > 0
    half = pl.ds(0, MEMBERS // 2), pl.ds(MEMBERS // 2, MEMBERS // 2)
    loads = [pltpu.make_async_copy(n_ref.at[part], own.at[part], load_sem.at[i]) for i, part in enumerate(half)]
    for item in loads:
        item.start()
    barrier = pltpu.get_barrier_semaphore()
    for peer in [(east, lat), (west, lat)] + [(i, j) for j in (north, south) for i in (lon, east, west)]:
        pl.semaphore_signal(barrier, inc=1, device_id=peer, device_id_type=MESH)


    def clear(part):
        size = part.size
        coef_beyond[:, :, part] = jnp.zeros((4, LEVELS, size, LANES), F32)
        beyond_west[:, part] = jnp.zeros((PAIRS, size, LANES), F32)
        beyond_east[:, part] = jnp.zeros((PAIRS, size, LANES), F32)

        @pl.loop(0, MEMBERS)
        def _(m):
            beyond[m, :, part] = jnp.zeros((LEVELS, size, LANES), F32)

    clear(pl.ds(2, TILE_LAT - 4))

    @pl.when(lat == 15)
    def _():
        clear(pl.ds(0, 2))

    @pl.when(lat == 0)
    def _():
        clear(pl.ds(TILE_LAT - 2, 2))

    lanes = lax.broadcasted_iota(jnp.int32, (TILE_LAT, LANES), 1)
    rows = lax.broadcasted_iota(jnp.int32, (TILE_LAT, LANES), 0)
    group, slot = lanes // 4, lax.rem(lanes, 4)
    is_first, is_last = rows == 0, rows == TILE_LAT - 1

    def packed(ref, part):
        out = jnp.zeros((ref[part, 0].shape[0], TILE_LAT, LANES), F32)
        for level in range(LEVELS):
            out = jnp.where(group == level, pltpu.roll(ref[part, level], (4 * level + 2) % LANES, 2), out)
        return out

    coef_edges[...] = packed(coefs, pl.ds(0, 4))
    for i, item in enumerate(loads):
        item.wait()
        edges[half[i]] = packed(own, half[i])
    first, second = edges[half[0]], edges[half[1]]
    to_east[...] = jnp.where(slot < 2, first, pltpu.roll(second, 2, 2))
    to_west[...] = jnp.where(slot >= 2, first, pltpu.roll(second, LANES - 2, 2))
    pl.semaphore_wait(barrier, 8)

    def copy(src, dst, send_sem, recv_sem, peer):
        return pltpu.make_async_remote_copy(
            src_ref=src, dst_ref=dst, send_sem=send_sem, recv_sem=recv_sem, device_id=peer, device_id_type=MESH
        )

    def small(i, src, dst, peer):
        return copy(src, dst, small_send.at[i], small_recv.at[i], peer)

    last, initial = pl.ds(TILE_LAT - 1, 1), pl.ds(0, 1)
    across = [
        small(0, coef_edges, coef_west, (east, lat)),
        small(1, coef_edges, coef_east, (west, lat)),
        small(2, to_east, edges_west, (east, lat)),
        small(3, to_west, edges_east, (west, lat)),
    ]
    up = [
        small(4, to_east.at[:, last], beyond_west.at[:, last], (east, north)),
        small(5, to_west.at[:, last], beyond_east.at[:, last], (west, north)),
        small(6, coefs.at[:, :, last], coef_beyond.at[:, :, last], (lon, north)),
    ]
    down = [
        small(7, to_east.at[:, initial], beyond_west.at[:, initial], (east, south)),
        small(8, to_west.at[:, initial], beyond_east.at[:, initial], (west, south)),
        small(9, coefs.at[:, :, initial], coef_beyond.at[:, :, initial], (lon, south)),
    ]

    def bulk_up(q):
        levels = pl.ds(q * CHUNK, CHUNK)
        part = pl.ds(TILE_LAT - 2, 2)
        return copy(n_ref.at[:, levels, part], beyond.at[:, levels, part], up_send.at[q], up_recv.at[q], (lon, north))

    def bulk_down(q):
        levels = pl.ds(q * CHUNK, CHUNK)
        part = pl.ds(0, 2)
        return copy(n_ref.at[:, levels, part], beyond.at[:, levels, part], down_send.at[q], down_recv.at[q], (lon, south))

    for item in across:
        item.start()

    @pl.when(has_north)
    def _():
        for item in up:
            item.start()

    @pl.when(has_south)
    def _():
        for item in down:
            item.start()

    for q in range(CHUNKS):

        @pl.when(has_north)
        def _():
            bulk_up(q).start()

        @pl.when(has_south)
        def _():
            bulk_down(q).start()

    for item in across:
        item.wait()

    @pl.when(has_south)
    def _():
        for item in up:
            item.wait_recv()

    @pl.when(has_north)
    def _():
        for item in down:
            item.wait_recv()

    def prepared(u, v, source, loss):
        keep = 1.0 - loss
        return keep * (1.0 - jnp.abs(u) - jnp.abs(v)), keep * jnp.abs(u), keep * jnp.abs(v), source, u > 0.0, v > 0.0

    def step(n, west_cell, east_cell, outside, prep):
        centre, along, across_, source, from_west, from_south = prep
        north_cell = pltpu.roll(jnp.where(is_first, outside, n), TILE_LAT - 1, 1)
        south_cell = pltpu.roll(jnp.where(is_last, outside, n), 1, 1)
        upwind_lon = jnp.where(from_west, west_cell, east_cell)
        upwind_lat = jnp.where(from_south, south_cell, north_cell)
        return centre * n + along * upwind_lon + across_ * upwind_lat + source

    def framed_step(n, frame, outside, prep):
        west_cell = pltpu.roll(jnp.where(lanes == LANES - 1, frame, n), 1, 2)
        east_cell = pltpu.roll(jnp.where(lanes == 0, frame, n), LANES - 1, 2)
        return step(n, west_cell, east_cell, outside, prep)

    edge_prep = prepared(*[jnp.where(slot == 1, coef_west[i], coef_east[i]) for i in range(4)])

    for i, part in enumerate(half):
        mine, from_west, from_east = edges[part], edges_west[...], edges_east[...]
        outside_west, outside_east = beyond_west[...], beyond_east[...]
        if i:
            from_west, outside_west = (pltpu.roll(v, LANES - 2, 2) for v in (from_west, outside_west))
            from_east, outside_east = (pltpu.roll(v, 2, 2) for v in (from_east, outside_east))
        frame = jnp.where(slot == 1, from_west, from_east)
        outside = jnp.where(slot == 1, outside_west, outside_east)
        west_cell = pltpu.roll(jnp.where(slot == 0, from_west, mine), 1, 2)
        east_cell = pltpu.roll(jnp.where(slot == 3, from_east, mine), LANES - 1, 2)
        frame0[part] = frame
        frame_beyond[part] = outside
        frame1[part] = step(frame, west_cell, east_cell, outside, edge_prep)
    total[...] = jnp.zeros_like(total)

    @pl.loop(0, CHUNKS)
    def _(q):
        @pl.when(has_south)
        def _():
            bulk_up(q).wait_recv()

        @pl.when(has_north)
        def _():
            bulk_down(q).wait_recv()

        @pl.loop(0, CHUNK)
        def _(i):
            level = q * CHUNK + i
            prep = prepared(*[coefs[k, level] for k in range(4)])
            prep_beyond = prepared(*[coef_beyond[k, level] for k in range(4)])
            shift = lax.rem(2 * LANES - 2 - 4 * level, LANES)

            @pl.loop(0, MEMBERS // BATCH)
            def _(g):
                part = pl.ds(g * BATCH, BATCH)
                n, out = own[part, level], beyond[part, level]
                n1 = framed_step(n, pltpu.roll(frame0[part], shift, 2), out, prep)
                out1 = framed_step(out, pltpu.roll(frame_beyond[part], shift, 2), n, prep_beyond)
                n2 = framed_step(n1, pltpu.roll(frame1[part], shift, 2), out1, prep)
                out_ref[part, level] = n2
                total[part] += n2

    flat = total.reshape(MEMBERS * TILE_LAT, LANES)
    for y in range(TILE_LAT):
        content_ref[y] = (flat[pl.ds(y, MEMBERS, stride=TILE_LAT), :] / math.sqrt(LEVELS)).astype(BF16)

    @pl.when(has_north)
    def _():
        for item in up:
            item.wait_send()
        for q in range(CHUNKS):
            bulk_up(q).wait_send()

    @pl.when(has_south)
    def _():
        for item in down:
            item.wait_send()
        for q in range(CHUNKS):
            bulk_down(q).wait_send()


def forecast(n, east_courant, north_courant, production, loss_rate):
    vmem = pl.BlockSpec(memory_space=VMEM)
    hbm = pl.BlockSpec(memory_space=pltpu.HBM)
    field = VMEM((MEMBERS, LEVELS, TILE_LAT, LANES), F32)
    packs = VMEM((MEMBERS, TILE_LAT, LANES), F32)
    pairs = VMEM((PAIRS, TILE_LAT, LANES), F32)
    coef_packs = VMEM((4, TILE_LAT, LANES), F32)
    dma = pltpu.SemaphoreType.DMA
    return pl.pallas_call(
        forecast_kernel,
        out_shape=(
            jax.ShapeDtypeStruct(n.shape, F32),
            jax.ShapeDtypeStruct((TILE_LAT, MEMBERS, LANES), BF16),
        ),
        in_specs=[vmem, hbm],
        out_specs=(vmem, vmem),
        scratch_shapes=[field] * 2
        + [packs] + [pairs] * 6
        + [coef_packs] * 3
        + [VMEM((4, LEVELS, TILE_LAT, LANES), F32)]
        + [packs] * 4
        + [dma((2,)), dma((10,)), dma((10,))]
        + [dma((CHUNKS,))] * 4,
        compiler_params=pltpu.CompilerParams(collective_id=2, has_side_effects=True, vmem_limit_bytes=46 * 2**20),
        name="forecast",
    )(jnp.stack([east_courant, north_courant, production, loss_rate]), n)


def ray_kernel(count_ref, row_ref, block_ref, content_ref, weight_ref, summed_ref, part_ref):
    summed_ref[...] = jnp.zeros_like(summed_ref)
    for k in range(SLOTS_TILE):
        picked = content_ref[row_ref[k]]
        part_ref[k] = jnp.dot(picked, weight_ref[k], preferred_element_type=F32)
    for k in range(SLOTS_TILE):
        block = block_ref[k]
        live = k < count_ref[0]
        summed_ref[block] += jnp.where(live, part_ref[k], 0.0)


def ray_sums(entry_count, entry_row, entry_block, content, path_weight):
    smem = pl.BlockSpec(memory_space=pltpu.SMEM)
    vmem = pl.BlockSpec(memory_space=VMEM)
    return pl.pallas_call(
        ray_kernel,
        out_shape=jax.ShapeDtypeStruct((COL_BLOCKS, MEMBERS, LANES), F32),
        in_specs=[smem, smem, smem, vmem, vmem],
        out_specs=vmem,
        scratch_shapes=[VMEM((SLOTS_TILE, MEMBERS, LANES), F32)],
        compiler_params=pltpu.CompilerParams(vmem_limit_bytes=16 * 2**20),
        name="ray_sums",
    )(entry_count, entry_row, entry_block, content, path_weight)


SWEEP = 8


def weights_from(total):
    rows = lax.broadcasted_iota(jnp.int32, (MEMBERS, LANES), 0)
    lanes = lax.broadcasted_iota(jnp.int32, (MEMBERS, LANES), 1)
    inverse_lanes = (lanes >= 64) & (lanes < 64 + MEMBERS)
    square = jnp.concatenate(
        [pltpu.roll(total[0:8], LANES - MEMBERS * k, 1) if k else total[0:8] for k in range(4)], axis=0
    )
    square = jnp.where(lanes < MEMBERS, square, 0.0)
    pull = jnp.sum(jnp.where(lanes == rows, total[8:9], 0.0), axis=1, keepdims=True)
    work = square + jnp.where(lanes == MEMBERS, pull, 0.0)
    work = work + jnp.where(lanes == rows, MEMBERS - 1.0, 0.0) + jnp.where(lanes == rows + 64, 1.0, 0.0)
    for start in range(0, MEMBERS, SWEEP):
        columns = [
            jnp.broadcast_to(work[:, j : j + 1], (MEMBERS, LANES)) for j in range(start, start + SWEEP)
        ]
        for k in range(SWEEP):
            j = start + k
            scale = jnp.where(rows > j, columns[k], 0.0) * (1.0 / columns[k][j : j + 1, :])
            for i in range(k + 1, SWEEP):
                columns[i] = columns[i] - scale * columns[i][j : j + 1, :]
            work = work - scale * work[j : j + 1, :]
    diagonal = jnp.sum(jnp.where(lanes == rows, work, 0.0), axis=1, keepdims=True)
    work = work / jnp.sqrt(diagonal)
    inverse = jnp.where(inverse_lanes, work, 0.0)
    halfway = work[:, MEMBERS : MEMBERS + 1]
    mean_weights = jnp.sum(inverse * halfway, axis=0, keepdims=True)
    transform = jnp.where(inverse_lanes, mean_weights + math.sqrt(MEMBERS - 1.0) * inverse, 0.0)
    rest = (1.0 - jnp.sum(transform, axis=1, keepdims=True)) * (1.0 / MEMBERS)
    return jnp.where(inverse_lanes, transform + rest, 0.0)


def analysis_kernel(
    summed_ref, observed_ref, var_ref, prior_ref, innovation_ref, weights_ref,
    own, from_core, from_x, half, from_z, g0, g1, g2, r_plane, r_y, r_z,
    own_sem, core_send, core_recv, x_send, x_recv, z_send, z_recv, a_send, a_recv,
):
    lon, lat = lax.axis_index("lon"), lax.axis_index("lat")
    x, z_hi, core = lat // 4, lax.rem(lat // 2, 2), lax.rem(lat, 2)
    z_lo, y = lon // 4, lax.rem(lon, 4)

    def x_peer(k):
        return (lon, lax.rem(lat + 4 * k, 16))

    def y_peer(k):
        return (z_lo * 4 + lax.rem(y + k, 4), lat)

    def z_peer(k):
        z = lax.rem(z_hi * 4 + z_lo + k, 8)
        return (lax.rem(z, 4) * 4 + y, x * 4 + (z // 4) * 2 + core)

    core_peer = (lon, lat + 1 - 2 * core)
    across = lat + 1 - 2 * core
    plane_peers = [core_peer] + [x_peer(k) for k in (1, 2, 3)]
    plane_peers += [(lon, lax.rem(across + 4 * k, 16)) for k in (1, 2, 3)]
    peers = plane_peers + [y_peer(k) for k in (1, 2, 3)]
    peers += [z_peer(k) for k in range(1, 8)]
    barrier = pltpu.get_barrier_semaphore()
    for peer in peers:
        pl.semaphore_signal(barrier, inc=1, device_id=peer, device_id_type=MESH)
    pieces = [(j, t) for t in (0, 1) for j in (2, 1, 3, 0)]

    def part_of(t):
        return z_hi if t else 1 - z_hi

    local = []
    for j, t in pieces:
        copy = pltpu.make_async_copy(
            summed_ref.at[lax.rem(x + j, 4), part_of(t), core], own.at[j, t], own_sem.at[j, t]
        )
        copy.start()
        local.append(copy)
    pl.semaphore_wait(barrier, len(peers))

    def send(src, dst, send_sem, recv_sem, peer):
        copy = pltpu.make_async_remote_copy(
            src_ref=src, dst_ref=dst, send_sem=send_sem, recv_sem=recv_sem, device_id=peer, device_id_type=MESH
        )
        copy.start()
        return copy

    core_copies = [
        send(
            summed_ref.at[lax.rem(x + j, 4), part_of(t), 1 - core], from_core.at[j, t],
            core_send.at[j, t], core_recv.at[j, t], core_peer,
        )
        for j, t in pieces
    ]
    x_copies = []
    for i, (j, t) in enumerate(pieces):
        local[i].wait()
        core_copies[i].wait_recv()
        own[j, t] = own[j, t] + from_core[j, t]
        if j:
            place = (j - 1, t)
            x_copies.append(send(own.at[j, t], from_x.at[place], x_send.at[place], x_recv.at[place], x_peer(j)))
    for copy in x_copies[:3]:
        copy.wait_recv()
    half[0] = own[0, 0] + from_x[0, 0] + from_x[1, 0] + from_x[2, 0]
    z_copy = send(half.at[0], from_z, z_send, z_recv, z_peer(4))
    for copy in x_copies[3:]:
        copy.wait_recv()
    half[1] = own[0, 1] + from_x[0, 1] + from_x[1, 1] + from_x[2, 1]
    z_copy.wait_recv()
    samples = half[1] + from_z[...]

    spreads, scaled = [], []
    for b in range(4):
        block = samples[b * MEMBERS : (b + 1) * MEMBERS]
        prior_ref[:, b * LANES : (b + 1) * LANES] = block
        mean = jnp.sum(block, axis=0, keepdims=True) * (1.0 / MEMBERS)
        misfit = observed_ref[b : b + 1, :] - mean
        variance = var_ref[b : b + 1, :]
        innovation_ref[b : b + 1, :] = misfit / jnp.sqrt(variance)
        spread = block - mean
        spreads.append(jnp.concatenate([spread, jnp.zeros((LANES - MEMBERS, LANES), F32)], axis=0))
        scaled.append(jnp.concatenate([spread, jnp.broadcast_to(misfit, (8, LANES))], axis=0) / variance)
    gram = lax.dot_general(
        jnp.concatenate(scaled, axis=1), jnp.concatenate(spreads, axis=1), (((1,), (1,)), ((), ())),
        precision=lax.Precision.HIGHEST, preferred_element_type=F32,
    )
    lanes = lax.broadcasted_iota(jnp.int32, gram.shape, 1)
    square = jnp.where(lanes < MEMBERS, gram, 0.0)
    g0[0:8] = sum(
        pltpu.roll(square[8 * k : 8 * k + 8], MEMBERS * k, 1) if k else square[0:8] for k in range(4)
    )
    g0[8:9] = gram[MEMBERS : MEMBERS + 1]

    waits = []
    base = 0

    def exchange(source, landing, targets):
        nonlocal base
        copies = [
            send(source, landing.at[i], a_send.at[base + i], a_recv.at[base + i], target)
            for i, target in enumerate(targets)
        ]
        base += len(targets)
        for copy in copies:
            copy.wait_recv()
        waits.extend(copies)
        total = source[...]
        for i in range(len(targets)):
            total = total + landing[i]
        return total

    g1[...] = exchange(g0, r_plane, plane_peers)
    g2[...] = exchange(g1, r_y, [y_peer(k) for k in (1, 2, 3)])
    total = exchange(g2, r_z, [z_peer(k) for k in range(1, 8)])
    weights_ref[...] = weights_from(total)
    for copy in core_copies + x_copies + [z_copy] + waits:
        copy.wait_send()


def analysis(summed, observed, obs_var):
    vmem = pl.BlockSpec(memory_space=VMEM)
    piece = (2, 4 * MEMBERS, LANES)
    dma = pltpu.SemaphoreType.DMA
    return pl.pallas_call(
        analysis_kernel,
        out_shape=(
            jax.ShapeDtypeStruct((MEMBERS, 4 * LANES), F32),
            jax.ShapeDtypeStruct((4, LANES), F32),
            jax.ShapeDtypeStruct((MEMBERS, LANES), F32),
        ),
        in_specs=[pl.BlockSpec(memory_space=pl.ANY), vmem, vmem],
        out_specs=(vmem, vmem, vmem),
        scratch_shapes=[
            VMEM((4,) + piece, F32), VMEM((4,) + piece, F32), VMEM((3,) + piece, F32), VMEM(piece, F32), VMEM(piece[1:], F32),
        ]
        + [VMEM((9, LANES), F32)] * 3
        + [VMEM((n, 9, LANES), F32) for n in (7, 3, 7)]
        + [dma((4, 2)), dma((4, 2)), dma((4, 2)), dma((3, 2)), dma((3, 2)), dma, dma, dma((17,)), dma((17,))],
        compiler_params=pltpu.CompilerParams(collective_id=1, has_side_effects=True, vmem_limit_bytes=16 * 2**20),
        name="analysis",
    )(summed.reshape(4, 2, 2, 4 * MEMBERS, LANES), observed.reshape(4, LANES), obs_var.reshape(4, LANES))


PART = 8
PARTS = LEVELS // PART


def update_kernel(
    weights_ref, prior_ref, innovation_ref, forecast_ref, out_ref, prior_out, innovation_out,
    high_ref, low_ref, updated_ref, store_sem,
):
    def store(i):
        levels = pl.ds(i * PART, PART)
        return pltpu.make_async_copy(updated_ref.at[:, levels], out_ref.at[:, levels], store_sem.at[i])

    prior_out[...] = prior_ref[...]
    innovation_out[...] = innovation_ref[...]
    size = MEMBERS * TILE_LAT
    tall = jnp.concatenate(
        [jnp.broadcast_to(weights_ref[b : b + 1, :], (TILE_LAT, LANES)) for b in range(MEMBERS)], axis=0
    )
    rows = lax.broadcasted_iota(jnp.int32, (LANES, size), 0)
    lanes = lax.broadcasted_iota(jnp.int32, (LANES, size), 1)
    spread = (lanes // TILE_LAT + 64 == rows).astype(BF16)
    r = lax.broadcasted_iota(jnp.int32, (size, size), 0)
    c = lax.broadcasted_iota(jnp.int32, (size, size), 1)
    same = lax.rem(r, TILE_LAT) == lax.rem(c, TILE_LAT)
    high = tall.astype(BF16)
    low = (tall - high.astype(F32)).astype(BF16)
    for part, ref in ((high, high_ref), (low, low_ref)):
        wide = jnp.dot(part, spread, preferred_element_type=F32)
        ref[...] = jnp.where(same, wide, 0.0).astype(BF16)

    for step in range(PARTS):
        for level in range(step * PART, (step + 1) * PART, 2):
            values = jnp.concatenate(
                [forecast_ref[:, level + i].reshape(MEMBERS * TILE_LAT, LANES) for i in range(2)], axis=1
            )
            high = values.astype(BF16)
            low = (values - high.astype(F32)).astype(BF16)
            out = jnp.dot(high_ref[...], high, preferred_element_type=F32)
            out += jnp.dot(high_ref[...], low, preferred_element_type=F32)
            out += jnp.dot(low_ref[...], high, preferred_element_type=F32)
            for i in range(2):
                updated_ref[:, level + i] = out[:, i * LANES : (i + 1) * LANES].reshape(MEMBERS, TILE_LAT, LANES)

        store(step).start()
    for i in range(PARTS):
        store(i).wait()


def update(weights, prior, innovation, forecast):
    size = MEMBERS * TILE_LAT
    vmem = pl.BlockSpec(memory_space=VMEM)
    hbm = pl.BlockSpec(memory_space=pltpu.HBM)
    field = VMEM(forecast.shape, F32)
    dma = pltpu.SemaphoreType.DMA
    return pl.pallas_call(
        update_kernel,
        out_shape=tuple(jax.ShapeDtypeStruct(v.shape, F32) for v in (forecast, prior, innovation)),
        in_specs=[vmem] * 4,
        out_specs=(hbm, vmem, vmem),
        scratch_shapes=[VMEM((size, size), BF16)] * 2 + [field, dma((PARTS,))],
        compiler_params=pltpu.CompilerParams(vmem_limit_bytes=24 * 2**20),
        name="update",
    )(weights, prior, innovation, forecast)


def per_device(
    sample_deviations, east_courant, north_courant, production, loss_rate,
    entry_count, entry_row, entry_block, path_weight, observed, obs_var,
):
    n, content = forecast(sample_deviations, east_courant, north_courant, production, loss_rate)
    summed = ray_sums(entry_count, entry_row, entry_block, content, path_weight)
    prior, innovation, weights = analysis(summed, observed, obs_var)
    updated, prior, innovation = update(weights, prior, innovation, n)
    return updated, prior, innovation.reshape(4 * LANES)


def solution(mesh):
    in_specs = (
        P(None, None, "lat", "lon"),
        P(None, "lat", "lon"),
        P(None, "lat", "lon"),
        P(None, "lat", "lon"),
        P(None, "lat", "lon"),
        P(("lon", "lat")),
        P(("lon", "lat")),
        P(("lon", "lat")),
        P(("lon", "lat"), None, None),
        P(("lon", "lat")),
        P(("lon", "lat")),
    )
    out_specs = (P(None, None, "lat", "lon"), P(None, ("lon", "lat")), P(("lon", "lat")))
    return jax.shard_map(per_device, mesh=mesh, in_specs=in_specs, out_specs=out_specs, check_vma=False)
```

```python
import math

import jax
import jax.numpy as jnp
from jax import lax
from jax.experimental import pallas as pl
from jax.experimental.pallas import tpu as pltpu
from jax.sharding import PartitionSpec as P

MEMBERS = 32
LEVELS = 32
TILE_LAT = 8
LANES = 128
SLOTS_TILE = 48
COL_BLOCKS = 64
MESH = pl.DeviceIdType.MESH
VMEM = pltpu.VMEM
F32 = jnp.float32
BF16 = jnp.bfloat16


CHUNKS = 8
CHUNK = LEVELS // CHUNKS
BATCH = 32
PAIRS = MEMBERS // 2
EARLY = 1


def forecast_kernel(
    coefs, n_ref, out_ref, content_ref,
    own, first, beyond, beyond_first, edge_coef, edges, to_east, to_west, edges_west, edges_east, beyond_west, beyond_east,
    coef_edges, coef_west, coef_east, coef_beyond, frame0, frame_beyond, frame1, total,
    load_sem, small_send, small_recv, up0, up0_recv, up1, up1_recv, down0, down0_recv, down1, down1_recv,
):
    lon, lat = lax.axis_index("lon"), lax.axis_index("lat")
    east, west = lax.rem(lon + 1, 16), lax.rem(lon + 15, 16)
    north, south = lax.rem(lat + 1, 16), lax.rem(lat + 15, 16)
    has_north, has_south = lat < 15, lat > 0
    half = pl.ds(0, MEMBERS // 2), pl.ds(MEMBERS // 2, MEMBERS // 2)
    loads = [pltpu.make_async_copy(n_ref.at[part], own.at[part], load_sem.at[i]) for i, part in enumerate(half)]
    for item in loads:
        item.start()
    barrier = pltpu.get_barrier_semaphore()
    for peer in [(east, lat), (west, lat)] + [(i, j) for j in (north, south) for i in (lon, east, west)]:
        pl.semaphore_signal(barrier, inc=1, device_id=peer, device_id_type=MESH)


    def clear(part):
        size = part.size
        coef_beyond[:, part] = jnp.zeros((LEVELS, size, LANES), F32)
        beyond_west[:, part] = jnp.zeros((PAIRS, size, LANES), F32)
        beyond_east[:, part] = jnp.zeros((PAIRS, size, LANES), F32)

        @pl.loop(0, MEMBERS)
        def _(m):
            beyond[m, :, part] = jnp.zeros((LEVELS, size, LANES), F32)
            beyond_first[m, :, part] = jnp.zeros((LEVELS, size, LANES), F32)

    clear(pl.ds(1, TILE_LAT - 2))

    @pl.when(lat == 15)
    def _():
        clear(pl.ds(0, 1))

    @pl.when(lat == 0)
    def _():
        clear(pl.ds(TILE_LAT - 1, 1))

    lanes = lax.broadcasted_iota(jnp.int32, (TILE_LAT, LANES), 1)
    rows = lax.broadcasted_iota(jnp.int32, (TILE_LAT, LANES), 0)
    group, slot = lanes // 4, lax.rem(lanes, 4)
    is_first, is_last = rows == 0, rows == TILE_LAT - 1

    def packed(ref, part):
        out = jnp.zeros((ref[part, 0].shape[0], TILE_LAT, LANES), F32)
        for level in range(LEVELS):
            out = jnp.where(group == level, pltpu.roll(ref[part, level], (4 * level + 2) % LANES, 2), out)
        return out

    coef_edges[...] = packed(coefs, pl.ds(0, 4))
    speed = coefs[1]
    leaves = (is_first & (speed > 0.0)) | (is_last & (speed < 0.0))
    edge_coef[...] = jnp.where(leaves, (1.0 - coefs[3]) * jnp.abs(speed), 0.0)
    for i, item in enumerate(loads):
        item.wait()
        edges[half[i]] = packed(own, half[i])
    front, back = edges[half[0]], edges[half[1]]
    to_east[...] = jnp.where(slot < 2, front, pltpu.roll(back, 2, 2))
    to_west[...] = jnp.where(slot >= 2, front, pltpu.roll(back, LANES - 2, 2))
    pl.semaphore_wait(barrier, 8)

    def copy(src, dst, send_sem, recv_sem, peer):
        return pltpu.make_async_remote_copy(
            src_ref=src, dst_ref=dst, send_sem=send_sem, recv_sem=recv_sem, device_id=peer, device_id_type=MESH
        )

    def small(i, src, dst, peer):
        return copy(src, dst, small_send.at[i], small_recv.at[i], peer)

    last, initial = pl.ds(TILE_LAT - 1, 1), pl.ds(0, 1)
    across = [
        small(0, coef_edges, coef_west, (east, lat)),
        small(1, coef_edges, coef_east, (west, lat)),
        small(2, to_east, edges_west, (east, lat)),
        small(3, to_west, edges_east, (west, lat)),
    ]
    up = [
        small(4, to_east.at[:, last], beyond_west.at[:, last], (east, north)),
        small(5, to_west.at[:, last], beyond_east.at[:, last], (west, north)),
        small(6, edge_coef.at[:, last], coef_beyond.at[:, last], (lon, north)),
    ]
    down = [
        small(7, to_east.at[:, initial], beyond_west.at[:, initial], (east, south)),
        small(8, to_west.at[:, initial], beyond_east.at[:, initial], (west, south)),
        small(9, edge_coef.at[:, initial], coef_beyond.at[:, initial], (lon, south)),
    ]

    def bulk(src, dst, q, row, send_sem, recv_sem, peer):
        levels = pl.ds(q * CHUNK, CHUNK)
        return copy(src.at[:, levels, row], dst.at[:, levels, row], send_sem.at[q], recv_sem.at[q], (lon, peer))

    fields = ((own, beyond), (first, beyond_first))
    up_sems = ((up0, up0_recv), (up1, up1_recv))
    down_sems = ((down0, down0_recv), (down1, down1_recv))

    def bulk_up(q, which):
        return bulk(*fields[which], q, last, *up_sems[which], north)

    def bulk_down(q, which):
        return bulk(*fields[which], q, initial, *down_sems[which], south)

    def start_bulk(q, which):
        @pl.when(has_north)
        def _():
            bulk_up(q, which).start()

        @pl.when(has_south)
        def _():
            bulk_down(q, which).start()

    for item in across:
        item.start()

    @pl.when(has_north)
    def _():
        for item in up:
            item.start()

    @pl.when(has_south)
    def _():
        for item in down:
            item.start()

    for q in range(EARLY):
        start_bulk(q, 0)

    for item in across:
        item.wait()

    for q in range(EARLY, CHUNKS):
        start_bulk(q, 0)

    @pl.when(has_south)
    def _():
        for item in up:
            item.wait_recv()

    @pl.when(has_north)
    def _():
        for item in down:
            item.wait_recv()

    def prepared(u, v, source, loss):
        keep = 1.0 - loss
        return keep * (1.0 - jnp.abs(u) - jnp.abs(v)), keep * jnp.abs(u), keep * jnp.abs(v), source, u > 0.0, v > 0.0

    def step(n, west_cell, east_cell, outside, prep):
        centre, along, across_, source, from_west, from_south = prep
        north_cell = pltpu.roll(jnp.where(is_first, outside, n), TILE_LAT - 1, 1)
        south_cell = pltpu.roll(jnp.where(is_last, outside, n), 1, 1)
        upwind_lon = jnp.where(from_west, west_cell, east_cell)
        upwind_lat = jnp.where(from_south, south_cell, north_cell)
        return centre * n + along * upwind_lon + across_ * upwind_lat + source

    def framed_step(n, frame, outside, prep):
        west_cell = pltpu.roll(jnp.where(lanes == LANES - 1, frame, n), 1, 2)
        east_cell = pltpu.roll(jnp.where(lanes == 0, frame, n), LANES - 1, 2)
        return step(n, west_cell, east_cell, outside, prep)

    edge_prep = prepared(*[jnp.where(slot == 1, coef_west[i], coef_east[i]) for i in range(4)])

    for i, part in enumerate(half):
        mine, from_west, from_east = edges[part], edges_west[...], edges_east[...]
        outside_west, outside_east = beyond_west[...], beyond_east[...]
        if i:
            from_west, outside_west = (pltpu.roll(v, LANES - 2, 2) for v in (from_west, outside_west))
            from_east, outside_east = (pltpu.roll(v, 2, 2) for v in (from_east, outside_east))
        frame = jnp.where(slot == 1, from_west, from_east)
        outside = jnp.where(slot == 1, outside_west, outside_east)
        west_cell = pltpu.roll(jnp.where(slot == 0, from_west, mine), 1, 2)
        east_cell = pltpu.roll(jnp.where(slot == 3, from_east, mine), LANES - 1, 2)
        frame0[part] = frame
        frame_beyond[part] = outside
        frame1[part] = step(frame, west_cell, east_cell, outside, edge_prep)
    total[...] = jnp.zeros_like(total)

    def level_prep(level):
        return prepared(*[coefs[k, level] for k in range(4)]), lax.rem(2 * LANES - 2 - 4 * level, LANES)

    def exchanged_rows(values):
        return jnp.where(is_first, pltpu.roll(values, 1, 1), pltpu.roll(values, TILE_LAT - 1, 1))

    @pl.loop(0, CHUNKS)
    def _(q):
        @pl.loop(0, CHUNK)
        def _(i):
            level = q * CHUNK + i
            prep, shift = level_prep(level)

            @pl.loop(0, MEMBERS // BATCH)
            def _(g):
                part = pl.ds(g * BATCH, BATCH)
                frame = pltpu.roll(frame0[part], shift, 2)
                first[part, level] = framed_step(own[part, level], frame, 0.0, prep)

        start_bulk(q, 1)

    @pl.loop(0, CHUNKS)
    def _(q):
        @pl.when(has_south)
        def _():
            for which in (0, 1):
                bulk_up(q, which).wait_recv()

        @pl.when(has_north)
        def _():
            for which in (0, 1):
                bulk_down(q, which).wait_recv()

        @pl.loop(0, CHUNK)
        def _(i):
            level = q * CHUNK + i
            prep, shift = level_prep(level)
            mine, theirs = edge_coef[level], coef_beyond[level]

            @pl.loop(0, MEMBERS // BATCH)
            def _(g):
                part = pl.ds(g * BATCH, BATCH)
                n1 = first[part, level] + mine * exchanged_rows(beyond[part, level])
                out1 = beyond_first[part, level] + theirs * exchanged_rows(own[part, level])
                n2 = framed_step(n1, pltpu.roll(frame1[part], shift, 2), out1, prep)
                out_ref[part, level] = n2
                total[part] += n2

    flat = total.reshape(MEMBERS * TILE_LAT, LANES)
    for y in range(TILE_LAT):
        content_ref[y] = (flat[pl.ds(y, MEMBERS, stride=TILE_LAT), :] / math.sqrt(LEVELS)).astype(BF16)

    @pl.when(has_north)
    def _():
        for item in up:
            item.wait_send()
        for q in range(CHUNKS):
            for which in (0, 1):
                bulk_up(q, which).wait_send()

    @pl.when(has_south)
    def _():
        for item in down:
            item.wait_send()
        for q in range(CHUNKS):
            for which in (0, 1):
                bulk_down(q, which).wait_send()


def forecast(n, east_courant, north_courant, production, loss_rate):
    vmem = pl.BlockSpec(memory_space=VMEM)
    hbm = pl.BlockSpec(memory_space=pltpu.HBM)
    field = VMEM((MEMBERS, LEVELS, TILE_LAT, LANES), F32)
    levels = VMEM((LEVELS, TILE_LAT, LANES), F32)
    packs = VMEM((MEMBERS, TILE_LAT, LANES), F32)
    pairs = VMEM((PAIRS, TILE_LAT, LANES), F32)
    coef_packs = VMEM((4, TILE_LAT, LANES), F32)
    dma = pltpu.SemaphoreType.DMA
    return pl.pallas_call(
        forecast_kernel,
        out_shape=(
            jax.ShapeDtypeStruct(n.shape, F32),
            jax.ShapeDtypeStruct((TILE_LAT, MEMBERS, LANES), BF16),
        ),
        in_specs=[vmem, hbm],
        out_specs=(vmem, vmem),
        scratch_shapes=[field] * 4
        + [levels]
        + [packs] + [pairs] * 6
        + [coef_packs] * 3
        + [levels]
        + [packs] * 4
        + [dma((2,)), dma((10,)), dma((10,))]
        + [dma((CHUNKS,))] * 8,
        compiler_params=pltpu.CompilerParams(collective_id=2, has_side_effects=True, vmem_limit_bytes=46 * 2**20),
        name="forecast",
    )(jnp.stack([east_courant, north_courant, production, loss_rate]), n)


def ray_kernel(count_ref, row_ref, block_ref, content_ref, weight_ref, summed_ref, part_ref):
    summed_ref[...] = jnp.zeros_like(summed_ref)
    for k in range(SLOTS_TILE):
        picked = content_ref[row_ref[k]]
        part_ref[k] = jnp.dot(picked, weight_ref[k], preferred_element_type=F32)
    for k in range(SLOTS_TILE):
        block = block_ref[k]
        live = k < count_ref[0]
        summed_ref[block] += jnp.where(live, part_ref[k], 0.0)


def ray_sums(entry_count, entry_row, entry_block, content, path_weight):
    smem = pl.BlockSpec(memory_space=pltpu.SMEM)
    vmem = pl.BlockSpec(memory_space=VMEM)
    return pl.pallas_call(
        ray_kernel,
        out_shape=jax.ShapeDtypeStruct((COL_BLOCKS, MEMBERS, LANES), F32),
        in_specs=[smem, smem, smem, vmem, vmem],
        out_specs=vmem,
        scratch_shapes=[VMEM((SLOTS_TILE, MEMBERS, LANES), F32)],
        compiler_params=pltpu.CompilerParams(vmem_limit_bytes=16 * 2**20),
        name="ray_sums",
    )(entry_count, entry_row, entry_block, content, path_weight)


SWEEP = 8


def weights_from(total):
    rows = lax.broadcasted_iota(jnp.int32, (MEMBERS, LANES), 0)
    lanes = lax.broadcasted_iota(jnp.int32, (MEMBERS, LANES), 1)
    inverse_lanes = (lanes >= 64) & (lanes < 64 + MEMBERS)
    square = jnp.concatenate(
        [pltpu.roll(total[0:8], LANES - MEMBERS * k, 1) if k else total[0:8] for k in range(4)], axis=0
    )
    square = jnp.where(lanes < MEMBERS, square, 0.0)
    pull = jnp.sum(jnp.where(lanes == rows, total[8:9], 0.0), axis=1, keepdims=True)
    work = square + jnp.where(lanes == MEMBERS, pull, 0.0)
    work = work + jnp.where(lanes == rows, MEMBERS - 1.0, 0.0) + jnp.where(lanes == rows + 64, 1.0, 0.0)
    for start in range(0, MEMBERS, SWEEP):
        columns = [
            jnp.broadcast_to(work[:, j : j + 1], (MEMBERS, LANES)) for j in range(start, start + SWEEP)
        ]
        for k in range(SWEEP):
            j = start + k
            scale = jnp.where(rows > j, columns[k], 0.0) * (1.0 / columns[k][j : j + 1, :])
            for i in range(k + 1, SWEEP):
                columns[i] = columns[i] - scale * columns[i][j : j + 1, :]
            work = work - scale * work[j : j + 1, :]
    diagonal = jnp.sum(jnp.where(lanes == rows, work, 0.0), axis=1, keepdims=True)
    work = work / jnp.sqrt(diagonal)
    inverse = jnp.where(inverse_lanes, work, 0.0)
    halfway = work[:, MEMBERS : MEMBERS + 1]
    mean_weights = jnp.sum(inverse * halfway, axis=0, keepdims=True)
    transform = jnp.where(inverse_lanes, mean_weights + math.sqrt(MEMBERS - 1.0) * inverse, 0.0)
    rest = (1.0 - jnp.sum(transform, axis=1, keepdims=True)) * (1.0 / MEMBERS)
    return jnp.where(inverse_lanes, transform + rest, 0.0)


def analysis_kernel(
    summed_ref, observed_ref, var_ref, prior_ref, innovation_ref, weights_ref,
    own, from_core, from_x, half, from_z, g0, g1, g2, r_plane, r_y, r_z,
    own_sem, core_send, core_recv, x_send, x_recv, z_send, z_recv, a_send, a_recv,
):
    lon, lat = lax.axis_index("lon"), lax.axis_index("lat")
    x, z_hi, core = lat // 4, lax.rem(lat // 2, 2), lax.rem(lat, 2)
    z_lo, y = lon // 4, lax.rem(lon, 4)

    def x_peer(k):
        return (lon, lax.rem(lat + 4 * k, 16))

    def y_peer(k):
        return (z_lo * 4 + lax.rem(y + k, 4), lat)

    def z_peer(k):
        z = lax.rem(z_hi * 4 + z_lo + k, 8)
        return (lax.rem(z, 4) * 4 + y, x * 4 + (z // 4) * 2 + core)

    core_peer = (lon, lat + 1 - 2 * core)
    across = lat + 1 - 2 * core
    plane_peers = [core_peer] + [x_peer(k) for k in (1, 2, 3)]
    plane_peers += [(lon, lax.rem(across + 4 * k, 16)) for k in (1, 2, 3)]
    peers = plane_peers + [y_peer(k) for k in (1, 2, 3)]
    peers += [z_peer(k) for k in range(1, 8)]
    barrier = pltpu.get_barrier_semaphore()
    for peer in peers:
        pl.semaphore_signal(barrier, inc=1, device_id=peer, device_id_type=MESH)
    pieces = [(j, t) for t in (0, 1) for j in (2, 1, 3, 0)]

    def part_of(t):
        return z_hi if t else 1 - z_hi

    local = []
    for j, t in pieces:
        copy = pltpu.make_async_copy(
            summed_ref.at[lax.rem(x + j, 4), part_of(t), core], own.at[j, t], own_sem.at[j, t]
        )
        copy.start()
        local.append(copy)
    pl.semaphore_wait(barrier, len(peers))

    def send(src, dst, send_sem, recv_sem, peer):
        copy = pltpu.make_async_remote_copy(
            src_ref=src, dst_ref=dst, send_sem=send_sem, recv_sem=recv_sem, device_id=peer, device_id_type=MESH
        )
        copy.start()
        return copy

    core_copies = [
        send(
            summed_ref.at[lax.rem(x + j, 4), part_of(t), 1 - core], from_core.at[j, t],
            core_send.at[j, t], core_recv.at[j, t], core_peer,
        )
        for j, t in pieces
    ]
    x_copies = []
    for i, (j, t) in enumerate(pieces):
        local[i].wait()
        core_copies[i].wait_recv()
        own[j, t] = own[j, t] + from_core[j, t]
        if j:
            place = (j - 1, t)
            x_copies.append(send(own.at[j, t], from_x.at[place], x_send.at[place], x_recv.at[place], x_peer(j)))
    for copy in x_copies[:3]:
        copy.wait_recv()
    half[0] = own[0, 0] + from_x[0, 0] + from_x[1, 0] + from_x[2, 0]
    z_copy = send(half.at[0], from_z, z_send, z_recv, z_peer(4))
    for copy in x_copies[3:]:
        copy.wait_recv()
    half[1] = own[0, 1] + from_x[0, 1] + from_x[1, 1] + from_x[2, 1]
    z_copy.wait_recv()
    samples = half[1] + from_z[...]

    spreads, scaled = [], []
    for b in range(4):
        block = samples[b * MEMBERS : (b + 1) * MEMBERS]
        prior_ref[:, b * LANES : (b + 1) * LANES] = block
        mean = jnp.sum(block, axis=0, keepdims=True) * (1.0 / MEMBERS)
        misfit = observed_ref[b : b + 1, :] - mean
        variance = var_ref[b : b + 1, :]
        innovation_ref[b : b + 1, :] = misfit / jnp.sqrt(variance)
        spread = block - mean
        spreads.append(jnp.concatenate([spread, jnp.zeros((LANES - MEMBERS, LANES), F32)], axis=0))
        scaled.append(jnp.concatenate([spread, jnp.broadcast_to(misfit, (8, LANES))], axis=0) / variance)
    gram = lax.dot_general(
        jnp.concatenate(scaled, axis=1), jnp.concatenate(spreads, axis=1), (((1,), (1,)), ((), ())),
        precision=lax.Precision.HIGHEST, preferred_element_type=F32,
    )
    lanes = lax.broadcasted_iota(jnp.int32, gram.shape, 1)
    square = jnp.where(lanes < MEMBERS, gram, 0.0)
    g0[0:8] = sum(
        pltpu.roll(square[8 * k : 8 * k + 8], MEMBERS * k, 1) if k else square[0:8] for k in range(4)
    )
    g0[8:9] = gram[MEMBERS : MEMBERS + 1]

    waits = []
    base = 0

    def exchange(source, landing, targets):
        nonlocal base
        copies = [
            send(source, landing.at[i], a_send.at[base + i], a_recv.at[base + i], target)
            for i, target in enumerate(targets)
        ]
        base += len(targets)
        for copy in copies:
            copy.wait_recv()
        waits.extend(copies)
        total = source[...]
        for i in range(len(targets)):
            total = total + landing[i]
        return total

    g1[...] = exchange(g0, r_plane, plane_peers)
    g2[...] = exchange(g1, r_y, [y_peer(k) for k in (1, 2, 3)])
    total = exchange(g2, r_z, [z_peer(k) for k in range(1, 8)])
    weights_ref[...] = weights_from(total)
    for copy in core_copies + x_copies + [z_copy] + waits:
        copy.wait_send()


def analysis(summed, observed, obs_var):
    vmem = pl.BlockSpec(memory_space=VMEM)
    piece = (2, 4 * MEMBERS, LANES)
    dma = pltpu.SemaphoreType.DMA
    return pl.pallas_call(
        analysis_kernel,
        out_shape=(
            jax.ShapeDtypeStruct((MEMBERS, 4 * LANES), F32),
            jax.ShapeDtypeStruct((4, LANES), F32),
            jax.ShapeDtypeStruct((MEMBERS, LANES), F32),
        ),
        in_specs=[pl.BlockSpec(memory_space=pl.ANY), vmem, vmem],
        out_specs=(vmem, vmem, vmem),
        scratch_shapes=[
            VMEM((4,) + piece, F32), VMEM((4,) + piece, F32), VMEM((3,) + piece, F32), VMEM(piece, F32), VMEM(piece[1:], F32),
        ]
        + [VMEM((9, LANES), F32)] * 3
        + [VMEM((n, 9, LANES), F32) for n in (7, 3, 7)]
        + [dma((4, 2)), dma((4, 2)), dma((4, 2)), dma((3, 2)), dma((3, 2)), dma, dma, dma((17,)), dma((17,))],
        compiler_params=pltpu.CompilerParams(collective_id=1, has_side_effects=True, vmem_limit_bytes=16 * 2**20),
        name="analysis",
    )(summed.reshape(4, 2, 2, 4 * MEMBERS, LANES), observed.reshape(4, LANES), obs_var.reshape(4, LANES))


PART = 8
PARTS = LEVELS // PART


def update_kernel(
    weights_ref, prior_ref, innovation_ref, forecast_ref, out_ref, prior_out, innovation_out,
    high_ref, low_ref, updated_ref, store_sem,
):
    def store(i):
        levels = pl.ds(i * PART, PART)
        return pltpu.make_async_copy(updated_ref.at[:, levels], out_ref.at[:, levels], store_sem.at[i])

    prior_out[...] = prior_ref[...]
    innovation_out[...] = innovation_ref[...]
    size = MEMBERS * TILE_LAT
    tall = jnp.concatenate(
        [jnp.broadcast_to(weights_ref[b : b + 1, :], (TILE_LAT, LANES)) for b in range(MEMBERS)], axis=0
    )
    rows = lax.broadcasted_iota(jnp.int32, (LANES, size), 0)
    lanes = lax.broadcasted_iota(jnp.int32, (LANES, size), 1)
    spread = (lanes // TILE_LAT + 64 == rows).astype(BF16)
    r = lax.broadcasted_iota(jnp.int32, (size, size), 0)
    c = lax.broadcasted_iota(jnp.int32, (size, size), 1)
    same = lax.rem(r, TILE_LAT) == lax.rem(c, TILE_LAT)
    high = tall.astype(BF16)
    low = (tall - high.astype(F32)).astype(BF16)
    for part, ref in ((high, high_ref), (low, low_ref)):
        wide = jnp.dot(part, spread, preferred_element_type=F32)
        ref[...] = jnp.where(same, wide, 0.0).astype(BF16)

    for step in range(PARTS):
        for level in range(step * PART, (step + 1) * PART, 2):
            values = jnp.concatenate(
                [forecast_ref[:, level + i].reshape(MEMBERS * TILE_LAT, LANES) for i in range(2)], axis=1
            )
            high = values.astype(BF16)
            low = (values - high.astype(F32)).astype(BF16)
            out = jnp.dot(high_ref[...], high, preferred_element_type=F32)
            out += jnp.dot(high_ref[...], low, preferred_element_type=F32)
            out += jnp.dot(low_ref[...], high, preferred_element_type=F32)
            for i in range(2):
                updated_ref[:, level + i] = out[:, i * LANES : (i + 1) * LANES].reshape(MEMBERS, TILE_LAT, LANES)

        store(step).start()
    for i in range(PARTS):
        store(i).wait()


def update(weights, prior, innovation, forecast):
    size = MEMBERS * TILE_LAT
    vmem = pl.BlockSpec(memory_space=VMEM)
    hbm = pl.BlockSpec(memory_space=pltpu.HBM)
    field = VMEM(forecast.shape, F32)
    dma = pltpu.SemaphoreType.DMA
    return pl.pallas_call(
        update_kernel,
        out_shape=tuple(jax.ShapeDtypeStruct(v.shape, F32) for v in (forecast, prior, innovation)),
        in_specs=[vmem] * 4,
        out_specs=(hbm, vmem, vmem),
        scratch_shapes=[VMEM((size, size), BF16)] * 2 + [field, dma((PARTS,))],
        compiler_params=pltpu.CompilerParams(vmem_limit_bytes=24 * 2**20),
        name="update",
    )(weights, prior, innovation, forecast)


def per_device(
    sample_deviations, east_courant, north_courant, production, loss_rate,
    entry_count, entry_row, entry_block, path_weight, observed, obs_var,
):
    n, content = forecast(sample_deviations, east_courant, north_courant, production, loss_rate)
    summed = ray_sums(entry_count, entry_row, entry_block, content, path_weight)
    prior, innovation, weights = analysis(summed, observed, obs_var)
    updated, prior, innovation = update(weights, prior, innovation, n)
    return updated, prior, innovation.reshape(4 * LANES)


def solution(mesh):
    in_specs = (
        P(None, None, "lat", "lon"),
        P(None, "lat", "lon"),
        P(None, "lat", "lon"),
        P(None, "lat", "lon"),
        P(None, "lat", "lon"),
        P(("lon", "lat")),
        P(("lon", "lat")),
        P(("lon", "lat")),
        P(("lon", "lat"), None, None),
        P(("lon", "lat")),
        P(("lon", "lat")),
    )
    out_specs = (P(None, None, "lat", "lon"), P(None, ("lon", "lat")), P(("lon", "lat")))
    return jax.shard_map(per_device, mesh=mesh, in_specs=in_specs, out_specs=out_specs, check_vma=False)
```

```python
import math

import jax
import jax.numpy as jnp
from jax import lax
from jax.experimental import pallas as pl
from jax.experimental.pallas import tpu as pltpu
from jax.sharding import PartitionSpec as P

MEMBERS = 32
LEVELS = 32
TILE_LAT = 8
LANES = 128
SLOTS_TILE = 48
COL_BLOCKS = 64
MESH = pl.DeviceIdType.MESH
VMEM = pltpu.VMEM
F32 = jnp.float32
BF16 = jnp.bfloat16


CHUNKS = 8
CHUNK = LEVELS // CHUNKS
BATCH = 32
PAIRS = MEMBERS // 2
EARLY = 1


def forecast_kernel(
    coefs, n_ref, out_ref, content_ref,
    own, first, beyond, beyond_first, edge_coef, edges, to_east, to_west, edges_west, edges_east, beyond_west, beyond_east,
    coef_edges, coef_west, coef_east, coef_beyond, frame0, frame_beyond, frame1, total,
    load_sem, small_send, small_recv, up0, up0_recv, up1, up1_recv, down0, down0_recv, down1, down1_recv,
):
    lon, lat = lax.axis_index("lon"), lax.axis_index("lat")
    east, west = lax.rem(lon + 1, 16), lax.rem(lon + 15, 16)
    north, south = lax.rem(lat + 1, 16), lax.rem(lat + 15, 16)
    has_north, has_south = lat < 15, lat > 0
    half = pl.ds(0, MEMBERS // 2), pl.ds(MEMBERS // 2, MEMBERS // 2)
    loads = [pltpu.make_async_copy(n_ref.at[part], own.at[part], load_sem.at[i]) for i, part in enumerate(half)]
    for item in loads:
        item.start()
    barrier = pltpu.get_barrier_semaphore()
    for peer in [(east, lat), (west, lat)] + [(i, j) for j in (north, south) for i in (lon, east, west)]:
        pl.semaphore_signal(barrier, inc=1, device_id=peer, device_id_type=MESH)


    def clear(part):
        size = part.size
        coef_beyond[:, part] = jnp.zeros((LEVELS, size, LANES), F32)
        beyond_west[:, part] = jnp.zeros((PAIRS, size, LANES), F32)
        beyond_east[:, part] = jnp.zeros((PAIRS, size, LANES), F32)

        @pl.loop(0, MEMBERS)
        def _(m):
            beyond[m, :, part] = jnp.zeros((LEVELS, size, LANES), F32)
            beyond_first[m, :, part] = jnp.zeros((LEVELS, size, LANES), F32)

    clear(pl.ds(1, TILE_LAT - 2))

    @pl.when(lat == 15)
    def _():
        clear(pl.ds(0, 1))

    @pl.when(lat == 0)
    def _():
        clear(pl.ds(TILE_LAT - 1, 1))

    lanes = lax.broadcasted_iota(jnp.int32, (TILE_LAT, LANES), 1)
    rows = lax.broadcasted_iota(jnp.int32, (TILE_LAT, LANES), 0)
    group, slot = lanes // 4, lax.rem(lanes, 4)
    is_first, is_last = rows == 0, rows == TILE_LAT - 1

    def packed(ref, part):
        out = jnp.zeros((ref[part, 0].shape[0], TILE_LAT, LANES), F32)
        for level in range(LEVELS):
            out = jnp.where(group == level, pltpu.roll(ref[part, level], (4 * level + 2) % LANES, 2), out)
        return out

    coef_edges[...] = packed(coefs, pl.ds(0, 4))
    speed = coefs[1]
    leaves = (is_first & (speed > 0.0)) | (is_last & (speed < 0.0))
    edge_coef[...] = jnp.where(leaves, (1.0 - coefs[3]) * jnp.abs(speed), 0.0)
    for i, item in enumerate(loads):
        item.wait()
        edges[half[i]] = packed(own, half[i])
    front, back = edges[half[0]], edges[half[1]]
    to_east[...] = jnp.where(slot < 2, front, pltpu.roll(back, 2, 2))
    to_west[...] = jnp.where(slot >= 2, front, pltpu.roll(back, LANES - 2, 2))
    pl.semaphore_wait(barrier, 8)

    def copy(src, dst, send_sem, recv_sem, peer):
        return pltpu.make_async_remote_copy(
            src_ref=src, dst_ref=dst, send_sem=send_sem, recv_sem=recv_sem, device_id=peer, device_id_type=MESH
        )

    def small(i, src, dst, peer):
        return copy(src, dst, small_send.at[i], small_recv.at[i], peer)

    last, initial = pl.ds(TILE_LAT - 1, 1), pl.ds(0, 1)
    across = [
        small(0, coef_edges, coef_west, (east, lat)),
        small(1, coef_edges, coef_east, (west, lat)),
        small(2, to_east, edges_west, (east, lat)),
        small(3, to_west, edges_east, (west, lat)),
    ]
    up = [
        small(4, to_east.at[:, last], beyond_west.at[:, last], (east, north)),
        small(5, to_west.at[:, last], beyond_east.at[:, last], (west, north)),
        small(6, edge_coef.at[:, last], coef_beyond.at[:, last], (lon, north)),
    ]
    down = [
        small(7, to_east.at[:, initial], beyond_west.at[:, initial], (east, south)),
        small(8, to_west.at[:, initial], beyond_east.at[:, initial], (west, south)),
        small(9, edge_coef.at[:, initial], coef_beyond.at[:, initial], (lon, south)),
    ]

    def bulk(src, dst, q, row, send_sem, recv_sem, peer):
        levels = pl.ds(q * CHUNK, CHUNK)
        return copy(src.at[:, levels, row], dst.at[:, levels, row], send_sem.at[q], recv_sem.at[q], (lon, peer))

    fields = ((own, beyond), (first, beyond_first))
    up_sems = ((up0, up0_recv), (up1, up1_recv))
    down_sems = ((down0, down0_recv), (down1, down1_recv))

    def bulk_up(q, which):
        return bulk(*fields[which], q, last, *up_sems[which], north)

    def bulk_down(q, which):
        return bulk(*fields[which], q, initial, *down_sems[which], south)

    def start_bulk(q, which):
        @pl.when(has_north)
        def _():
            bulk_up(q, which).start()

        @pl.when(has_south)
        def _():
            bulk_down(q, which).start()

    for item in across:
        item.start()

    @pl.when(has_north)
    def _():
        for item in up:
            item.start()

    @pl.when(has_south)
    def _():
        for item in down:
            item.start()

    for q in range(EARLY):
        start_bulk(q, 0)

    for item in across:
        item.wait()

    for q in range(EARLY, CHUNKS):
        start_bulk(q, 0)

    @pl.when(has_south)
    def _():
        for item in up:
            item.wait_recv()

    @pl.when(has_north)
    def _():
        for item in down:
            item.wait_recv()

    def prepared(u, v, source, loss):
        keep = 1.0 - loss
        return keep * (1.0 - jnp.abs(u) - jnp.abs(v)), keep * jnp.abs(u), keep * jnp.abs(v), source, u > 0.0, v > 0.0

    def step(n, west_cell, east_cell, outside, prep):
        centre, along, across_, source, from_west, from_south = prep
        north_cell = pltpu.roll(jnp.where(is_first, outside, n), TILE_LAT - 1, 1)
        south_cell = pltpu.roll(jnp.where(is_last, outside, n), 1, 1)
        upwind_lon = jnp.where(from_west, west_cell, east_cell)
        upwind_lat = jnp.where(from_south, south_cell, north_cell)
        return centre * n + along * upwind_lon + across_ * upwind_lat + source

    def framed_step(n, frame, outside, prep):
        west_cell = pltpu.roll(jnp.where(lanes == LANES - 1, frame, n), 1, 2)
        east_cell = pltpu.roll(jnp.where(lanes == 0, frame, n), LANES - 1, 2)
        return step(n, west_cell, east_cell, outside, prep)

    edge_prep = prepared(*[jnp.where(slot == 1, coef_west[i], coef_east[i]) for i in range(4)])

    for i, part in enumerate(half):
        mine, from_west, from_east = edges[part], edges_west[...], edges_east[...]
        outside_west, outside_east = beyond_west[...], beyond_east[...]
        if i:
            from_west, outside_west = (pltpu.roll(v, LANES - 2, 2) for v in (from_west, outside_west))
            from_east, outside_east = (pltpu.roll(v, 2, 2) for v in (from_east, outside_east))
        frame = jnp.where(slot == 1, from_west, from_east)
        outside = jnp.where(slot == 1, outside_west, outside_east)
        west_cell = pltpu.roll(jnp.where(slot == 0, from_west, mine), 1, 2)
        east_cell = pltpu.roll(jnp.where(slot == 3, from_east, mine), LANES - 1, 2)
        frame0[part] = frame
        frame_beyond[part] = outside
        frame1[part] = step(frame, west_cell, east_cell, outside, edge_prep)
    total[...] = jnp.zeros_like(total)

    def level_prep(level):
        return prepared(*[coefs[k, level] for k in range(4)]), lax.rem(2 * LANES - 2 - 4 * level, LANES)

    def exchanged_rows(values):
        return jnp.where(is_first, pltpu.roll(values, 1, 1), pltpu.roll(values, TILE_LAT - 1, 1))

    @pl.loop(0, CHUNKS)
    def _(q):
        @pl.loop(0, CHUNK)
        def _(i):
            level = q * CHUNK + i
            prep, shift = level_prep(level)

            @pl.loop(0, MEMBERS // BATCH)
            def _(g):
                part = pl.ds(g * BATCH, BATCH)
                frame = pltpu.roll(frame0[part], shift, 2)
                first[part, level] = framed_step(own[part, level], frame, 0.0, prep)

        start_bulk(q, 1)

    @pl.loop(0, CHUNKS)
    def _(q):
        @pl.when(has_south)
        def _():
            for which in (0, 1):
                bulk_up(q, which).wait_recv()

        @pl.when(has_north)
        def _():
            for which in (0, 1):
                bulk_down(q, which).wait_recv()

        @pl.loop(0, CHUNK)
        def _(i):
            level = q * CHUNK + i
            prep, shift = level_prep(level)
            mine, theirs = edge_coef[level], coef_beyond[level]

            @pl.loop(0, MEMBERS // BATCH)
            def _(g):
                part = pl.ds(g * BATCH, BATCH)
                n1 = first[part, level] + mine * exchanged_rows(beyond[part, level])
                out1 = beyond_first[part, level] + theirs * exchanged_rows(own[part, level])
                n2 = framed_step(n1, pltpu.roll(frame1[part], shift, 2), out1, prep)
                out_ref[part, level] = n2
                total[part] += n2

    flat = total.reshape(MEMBERS * TILE_LAT, LANES)
    for y in range(TILE_LAT):
        content_ref[y] = (flat[pl.ds(y, MEMBERS, stride=TILE_LAT), :] / math.sqrt(LEVELS)).astype(BF16)

    @pl.when(has_north)
    def _():
        for item in up:
            item.wait_send()
        for q in range(CHUNKS):
            for which in (0, 1):
                bulk_up(q, which).wait_send()

    @pl.when(has_south)
    def _():
        for item in down:
            item.wait_send()
        for q in range(CHUNKS):
            for which in (0, 1):
                bulk_down(q, which).wait_send()


def forecast(n, east_courant, north_courant, production, loss_rate):
    vmem = pl.BlockSpec(memory_space=VMEM)
    hbm = pl.BlockSpec(memory_space=pltpu.HBM)
    field = VMEM((MEMBERS, LEVELS, TILE_LAT, LANES), F32)
    levels = VMEM((LEVELS, TILE_LAT, LANES), F32)
    packs = VMEM((MEMBERS, TILE_LAT, LANES), F32)
    pairs = VMEM((PAIRS, TILE_LAT, LANES), F32)
    coef_packs = VMEM((4, TILE_LAT, LANES), F32)
    dma = pltpu.SemaphoreType.DMA
    return pl.pallas_call(
        forecast_kernel,
        out_shape=(
            jax.ShapeDtypeStruct(n.shape, F32),
            jax.ShapeDtypeStruct((TILE_LAT, MEMBERS, LANES), BF16),
        ),
        in_specs=[vmem, hbm],
        out_specs=(vmem, vmem),
        scratch_shapes=[field] * 4
        + [levels]
        + [packs] + [pairs] * 6
        + [coef_packs] * 3
        + [levels]
        + [packs] * 4
        + [dma((2,)), dma((10,)), dma((10,))]
        + [dma((CHUNKS,))] * 8,
        compiler_params=pltpu.CompilerParams(collective_id=2, has_side_effects=True, vmem_limit_bytes=46 * 2**20),
        name="forecast",
    )(jnp.stack([east_courant, north_courant, production, loss_rate]), n)


def ray_kernel(count_ref, row_ref, block_ref, content_ref, weight_ref, summed_ref, part_ref):
    summed_ref[...] = jnp.zeros_like(summed_ref)
    for k in range(SLOTS_TILE):
        picked = content_ref[row_ref[k]]
        part_ref[k] = jnp.dot(picked, weight_ref[k], preferred_element_type=F32)
    for k in range(SLOTS_TILE):
        block = block_ref[k]
        live = k < count_ref[0]
        summed_ref[block] += jnp.where(live, part_ref[k], 0.0)


def ray_sums(entry_count, entry_row, entry_block, content, path_weight):
    smem = pl.BlockSpec(memory_space=pltpu.SMEM)
    vmem = pl.BlockSpec(memory_space=VMEM)
    return pl.pallas_call(
        ray_kernel,
        out_shape=jax.ShapeDtypeStruct((COL_BLOCKS, MEMBERS, LANES), F32),
        in_specs=[smem, smem, smem, vmem, vmem],
        out_specs=vmem,
        scratch_shapes=[VMEM((SLOTS_TILE, MEMBERS, LANES), F32)],
        compiler_params=pltpu.CompilerParams(vmem_limit_bytes=16 * 2**20),
        name="ray_sums",
    )(entry_count, entry_row, entry_block, content, path_weight)


SWEEP = 8


def weights_from(total):
    rows = lax.broadcasted_iota(jnp.int32, (MEMBERS, LANES), 0)
    lanes = lax.broadcasted_iota(jnp.int32, (MEMBERS, LANES), 1)
    inverse_lanes = (lanes >= 64) & (lanes < 64 + MEMBERS)
    square = jnp.concatenate(
        [pltpu.roll(total[0:8], LANES - MEMBERS * k, 1) if k else total[0:8] for k in range(4)], axis=0
    )
    square = jnp.where(lanes < MEMBERS, square, 0.0)
    pull = jnp.sum(jnp.where(lanes == rows, total[8:9], 0.0), axis=1, keepdims=True)
    work = square + jnp.where(lanes == MEMBERS, pull, 0.0)
    work = work + jnp.where(lanes == rows, MEMBERS - 1.0, 0.0) + jnp.where(lanes == rows + 64, 1.0, 0.0)
    for start in range(0, MEMBERS, SWEEP):
        columns = [
            jnp.broadcast_to(work[:, j : j + 1], (MEMBERS, LANES)) for j in range(start, start + SWEEP)
        ]
        for k in range(SWEEP):
            j = start + k
            scale = jnp.where(rows > j, columns[k], 0.0) * (1.0 / columns[k][j : j + 1, :])
            for i in range(k + 1, SWEEP):
                columns[i] = columns[i] - scale * columns[i][j : j + 1, :]
            work = work - scale * work[j : j + 1, :]
    diagonal = jnp.sum(jnp.where(lanes == rows, work, 0.0), axis=1, keepdims=True)
    work = work / jnp.sqrt(diagonal)
    inverse = jnp.where(inverse_lanes, work, 0.0)
    halfway = work[:, MEMBERS : MEMBERS + 1]
    mean_weights = jnp.sum(inverse * halfway, axis=0, keepdims=True)
    transform = jnp.where(inverse_lanes, mean_weights + math.sqrt(MEMBERS - 1.0) * inverse, 0.0)
    rest = (1.0 - jnp.sum(transform, axis=1, keepdims=True)) * (1.0 / MEMBERS)
    return jnp.where(inverse_lanes, transform + rest, 0.0)


def analysis_kernel(
    summed_ref, observed_ref, var_ref, prior_ref, innovation_ref, weights_ref,
    own, from_core, from_x, half, from_z, g0, g1, g2, r_plane, r_y, r_z,
    own_sem, core_send, core_recv, x_send, x_recv, z_send, z_recv, a_send, a_recv,
):
    lon, lat = lax.axis_index("lon"), lax.axis_index("lat")
    x, z_hi, core = lat // 4, lax.rem(lat // 2, 2), lax.rem(lat, 2)
    z_lo, y = lon // 4, lax.rem(lon, 4)

    def x_peer(k):
        return (lon, lax.rem(lat + 4 * k, 16))

    def y_peer(k):
        return (z_lo * 4 + lax.rem(y + k, 4), lat)

    def z_peer(k):
        z = lax.rem(z_hi * 4 + z_lo + k, 8)
        return (lax.rem(z, 4) * 4 + y, x * 4 + (z // 4) * 2 + core)

    core_peer = (lon, lat + 1 - 2 * core)
    across = lat + 1 - 2 * core
    plane_peers = [core_peer] + [x_peer(k) for k in (1, 2, 3)]
    plane_peers += [(lon, lax.rem(across + 4 * k, 16)) for k in (1, 2, 3)]
    peers = plane_peers + [y_peer(k) for k in (1, 2, 3)]
    peers += [z_peer(k) for k in range(1, 8)]
    barrier = pltpu.get_barrier_semaphore()
    for peer in peers:
        pl.semaphore_signal(barrier, inc=1, device_id=peer, device_id_type=MESH)
    pieces = [(j, t) for t in (0, 1) for j in (2, 1, 3, 0)]

    def part_of(t):
        return z_hi if t else 1 - z_hi

    local = []
    for j, t in pieces:
        copy = pltpu.make_async_copy(
            summed_ref.at[lax.rem(x + j, 4), part_of(t), core], own.at[j, t], own_sem.at[j, t]
        )
        copy.start()
        local.append(copy)
    pl.semaphore_wait(barrier, len(peers))

    def send(src, dst, send_sem, recv_sem, peer):
        copy = pltpu.make_async_remote_copy(
            src_ref=src, dst_ref=dst, send_sem=send_sem, recv_sem=recv_sem, device_id=peer, device_id_type=MESH
        )
        copy.start()
        return copy

    core_copies = [
        send(
            summed_ref.at[lax.rem(x + j, 4), part_of(t), 1 - core], from_core.at[j, t],
            core_send.at[j, t], core_recv.at[j, t], core_peer,
        )
        for j, t in pieces
    ]
    x_copies = []
    for i, (j, t) in enumerate(pieces):
        local[i].wait()
        core_copies[i].wait_recv()
        own[j, t] = own[j, t] + from_core[j, t]
        if j:
            place = (j - 1, t)
            x_copies.append(send(own.at[j, t], from_x.at[place], x_send.at[place], x_recv.at[place], x_peer(j)))
    for copy in x_copies[:3]:
        copy.wait_recv()
    half[0] = own[0, 0] + from_x[0, 0] + from_x[1, 0] + from_x[2, 0]
    z_copy = send(half.at[0], from_z, z_send, z_recv, z_peer(4))
    for copy in x_copies[3:]:
        copy.wait_recv()
    half[1] = own[0, 1] + from_x[0, 1] + from_x[1, 1] + from_x[2, 1]
    z_copy.wait_recv()
    samples = half[1] + from_z[...]

    spreads, scaled = [], []
    for b in range(4):
        block = samples[b * MEMBERS : (b + 1) * MEMBERS]
        prior_ref[:, b * LANES : (b + 1) * LANES] = block
        mean = jnp.sum(block, axis=0, keepdims=True) * (1.0 / MEMBERS)
        misfit = observed_ref[b : b + 1, :] - mean
        variance = var_ref[b : b + 1, :]
        innovation_ref[b : b + 1, :] = misfit / jnp.sqrt(variance)
        spread = block - mean
        spreads.append(jnp.concatenate([spread, jnp.zeros((LANES - MEMBERS, LANES), F32)], axis=0))
        scaled.append(jnp.concatenate([spread, jnp.broadcast_to(misfit, (8, LANES))], axis=0) / variance)
    gram = lax.dot_general(
        jnp.concatenate(scaled, axis=1), jnp.concatenate(spreads, axis=1), (((1,), (1,)), ((), ())),
        precision=lax.Precision.HIGHEST, preferred_element_type=F32,
    )
    lanes = lax.broadcasted_iota(jnp.int32, gram.shape, 1)
    square = jnp.where(lanes < MEMBERS, gram, 0.0)
    g0[0:8] = sum(
        pltpu.roll(square[8 * k : 8 * k + 8], MEMBERS * k, 1) if k else square[0:8] for k in range(4)
    )
    g0[8:16] = gram[MEMBERS : MEMBERS + 8]

    waits = []
    base = 0

    def exchange(source, landing, targets):
        nonlocal base
        copies = [
            send(source, landing.at[i], a_send.at[base + i], a_recv.at[base + i], target)
            for i, target in enumerate(targets)
        ]
        base += len(targets)
        for copy in copies:
            copy.wait_recv()
        waits.extend(copies)
        total = source[...]
        for i in range(len(targets)):
            total = total + landing[i]
        return total

    g1[...] = exchange(g0, r_plane, plane_peers)
    g2[...] = exchange(g1, r_y, [y_peer(k) for k in (1, 2, 3)])
    total = exchange(g2, r_z, [z_peer(k) for k in range(1, 8)])
    weights_ref[...] = weights_from(total)
    for copy in core_copies + x_copies + [z_copy] + waits:
        copy.wait_send()


def analysis(summed, observed, obs_var):
    vmem = pl.BlockSpec(memory_space=VMEM)
    piece = (2, 4 * MEMBERS, LANES)
    dma = pltpu.SemaphoreType.DMA
    return pl.pallas_call(
        analysis_kernel,
        out_shape=(
            jax.ShapeDtypeStruct((MEMBERS, 4 * LANES), F32),
            jax.ShapeDtypeStruct((4, LANES), F32),
            jax.ShapeDtypeStruct((MEMBERS, LANES), F32),
        ),
        in_specs=[pl.BlockSpec(memory_space=pl.ANY), vmem, vmem],
        out_specs=(vmem, vmem, vmem),
        scratch_shapes=[
            VMEM((4,) + piece, F32), VMEM((4,) + piece, F32), VMEM((3,) + piece, F32), VMEM(piece, F32), VMEM(piece[1:], F32),
        ]
        + [VMEM((16, LANES), F32)] * 3
        + [VMEM((n, 16, LANES), F32) for n in (7, 3, 7)]
        + [dma((4, 2)), dma((4, 2)), dma((4, 2)), dma((3, 2)), dma((3, 2)), dma, dma, dma((17,)), dma((17,))],
        compiler_params=pltpu.CompilerParams(collective_id=1, has_side_effects=True, vmem_limit_bytes=16 * 2**20),
        name="analysis",
    )(summed.reshape(4, 2, 2, 4 * MEMBERS, LANES), observed.reshape(4, LANES), obs_var.reshape(4, LANES))


PART = 8
PARTS = LEVELS // PART


def update_kernel(
    weights_ref, prior_ref, innovation_ref, forecast_ref, out_ref, prior_out, innovation_out,
    high_ref, low_ref, updated_ref, store_sem,
):
    def store(i):
        levels = pl.ds(i * PART, PART)
        return pltpu.make_async_copy(updated_ref.at[:, levels], out_ref.at[:, levels], store_sem.at[i])

    prior_out[...] = prior_ref[...]
    innovation_out[...] = innovation_ref[...]
    size = MEMBERS * TILE_LAT
    tall = jnp.concatenate(
        [jnp.broadcast_to(weights_ref[b : b + 1, :], (TILE_LAT, LANES)) for b in range(MEMBERS)], axis=0
    )
    rows = lax.broadcasted_iota(jnp.int32, (LANES, size), 0)
    lanes = lax.broadcasted_iota(jnp.int32, (LANES, size), 1)
    spread = (lanes // TILE_LAT + 64 == rows).astype(BF16)
    r = lax.broadcasted_iota(jnp.int32, (size, size), 0)
    c = lax.broadcasted_iota(jnp.int32, (size, size), 1)
    same = lax.rem(r, TILE_LAT) == lax.rem(c, TILE_LAT)
    high = tall.astype(BF16)
    low = (tall - high.astype(F32)).astype(BF16)
    for part, ref in ((high, high_ref), (low, low_ref)):
        wide = jnp.dot(part, spread, preferred_element_type=F32)
        ref[...] = jnp.where(same, wide, 0.0).astype(BF16)

    for step in range(PARTS):
        for level in range(step * PART, (step + 1) * PART, 2):
            values = jnp.concatenate(
                [forecast_ref[:, level + i].reshape(MEMBERS * TILE_LAT, LANES) for i in range(2)], axis=1
            )
            high = values.astype(BF16)
            low = (values - high.astype(F32)).astype(BF16)
            out = jnp.dot(high_ref[...], high, preferred_element_type=F32)
            out += jnp.dot(high_ref[...], low, preferred_element_type=F32)
            out += jnp.dot(low_ref[...], high, preferred_element_type=F32)
            for i in range(2):
                updated_ref[:, level + i] = out[:, i * LANES : (i + 1) * LANES].reshape(MEMBERS, TILE_LAT, LANES)

        store(step).start()
    for i in range(PARTS):
        store(i).wait()


def update(weights, prior, innovation, forecast):
    size = MEMBERS * TILE_LAT
    vmem = pl.BlockSpec(memory_space=VMEM)
    hbm = pl.BlockSpec(memory_space=pltpu.HBM)
    field = VMEM(forecast.shape, F32)
    dma = pltpu.SemaphoreType.DMA
    return pl.pallas_call(
        update_kernel,
        out_shape=tuple(jax.ShapeDtypeStruct(v.shape, F32) for v in (forecast, prior, innovation)),
        in_specs=[vmem] * 4,
        out_specs=(hbm, vmem, vmem),
        scratch_shapes=[VMEM((size, size), BF16)] * 2 + [field, dma((PARTS,))],
        compiler_params=pltpu.CompilerParams(vmem_limit_bytes=24 * 2**20),
        name="update",
    )(weights, prior, innovation, forecast)


def per_device(
    sample_deviations, east_courant, north_courant, production, loss_rate,
    entry_count, entry_row, entry_block, path_weight, observed, obs_var,
):
    n, content = forecast(sample_deviations, east_courant, north_courant, production, loss_rate)
    summed = ray_sums(entry_count, entry_row, entry_block, content, path_weight)
    prior, innovation, weights = analysis(summed, observed, obs_var)
    updated, prior, innovation = update(weights, prior, innovation, n)
    return updated, prior, innovation.reshape(4 * LANES)


def solution(mesh):
    in_specs = (
        P(None, None, "lat", "lon"),
        P(None, "lat", "lon"),
        P(None, "lat", "lon"),
        P(None, "lat", "lon"),
        P(None, "lat", "lon"),
        P(("lon", "lat")),
        P(("lon", "lat")),
        P(("lon", "lat")),
        P(("lon", "lat"), None, None),
        P(("lon", "lat")),
        P(("lon", "lat")),
    )
    out_specs = (P(None, None, "lat", "lon"), P(None, ("lon", "lat")), P(("lon", "lat")))
    return jax.shard_map(per_device, mesh=mesh, in_specs=in_specs, out_specs=out_specs, check_vma=False)
```
